128 devices in a mesh: dp: 8 (over y, core), sp: 2 (over z_hi), tp: 8 (over x, z_lo).
Axes of the slice: x: 4, y: 4, z: 4 (z_hi: 2, z_lo: 2; z = z_hi * 2 + z_lo), core: 2. Of those that a mesh axis runs over, the one named last changes fastest.
Arguments:
- tokens: bfloat16 [16384, 2048], P(('dp', 'sp')), may hold values from -6 to 6
- cotangent: bfloat16 [16384, 2048], P(('dp', 'sp')), may hold values from -6 to 6
- seq_lens: int32 [8, 2], P('dp'), may hold values from 0 to 2048, as said below
- owners: int32 [4, 16], replicated, may hold values from 0 to 15, each once within a row
- shared_vec: float32 [6, 2048], replicated, may hold values from -1.5 to 1.6
- shared_first: float32 [6, 2048], replicated, may hold values from -768 to 768
- shared_second: float32 [6, 2048], replicated, may hold values from 16384 to 65536
- split_vec: float32 [8, 1792], P('tp'), may hold values from -0.75 to 0.75
- split_first: float32 [8, 1792], P('tp'), may hold values from -384 to 384
- split_second: float32 [8, 1792], P('tp'), may hold values from 4096 to 16384
- qkv_master: float32 [16, 128, 6144], P(('dp', 'sp'), None, 'tp'), may hold values from -0.125 to 0.125
- qkv_first: float32 [16, 128, 6144], P(('dp', 'sp'), None, 'tp'), may hold values from -1536 to 1536
- qkv_second: float32 [16, 128, 6144], P(('dp', 'sp'), None, 'tp'), may hold values from 65536 to 262144
- qkv_left: float32 [16, 8, 128, 128], P(('dp', 'sp'), 'tp'), may hold values from -1 to 1, as said below
- qkv_right: float32 [16, 8, 768, 768], P(('dp', 'sp'), 'tp'), may hold values from -1 to 1, as said below
- out_master: float32 [2048, 16, 128], P('tp', ('dp', 'sp')), may hold values from -1.5 to 1.5
- out_first: float32 [2048, 16, 128], P('tp', ('dp', 'sp')), may hold values from -80 to 80
- out_second: float32 [2048, 16, 128], P('tp', ('dp', 'sp')), may hold values from 163.84 to 655.36
- out_left: float32 [16, 8, 256, 256], P(('dp', 'sp'), 'tp'), may hold values from -1 to 1, as said below
- out_right: float32 [16, 8, 128, 128], P(('dp', 'sp'), 'tp'), may hold values from -1 to 1, as said below
- up_master: float32 [16, 128, 8192], P(('dp', 'sp'), None, 'tp'), may hold values from -0.125 to 0.125
- up_first: float32 [16, 128, 8192], P(('dp', 'sp'), None, 'tp'), may hold values from -224 to 224
- up_second: float32 [16, 128, 8192], P(('dp', 'sp'), None, 'tp'), may hold values from 1474.56 to 5898.24
- up_left: float32 [16, 8, 128, 128], P(('dp', 'sp'), 'tp'), may hold values from -1 to 1, as said below
- up_right: float32 [16, 8, 1024, 1024], P(('dp', 'sp'), 'tp'), may hold values from -1 to 1, as said below
- down_master: float32 [8192, 16, 128], P('tp', ('dp', 'sp')), may hold values from -0.0625 to 0.0625
- down_first: float32 [8192, 16, 128], P('tp', ('dp', 'sp')), may hold values from -448 to 448
- down_second: float32 [8192, 16, 128], P('tp', ('dp', 'sp')), may hold values from 5898.24 to 23592.96
- down_left: float32 [16, 8, 1024, 1024], P(('dp', 'sp'), 'tp'), may hold values from -1 to 1, as said below
- down_right: float32 [16, 8, 128, 128], P(('dp', 'sp'), 'tp'), may hold values from -1 to 1, as said below
Outputs:
- output: bfloat16 [16384, 2048], P(('dp', 'sp'))
- grad_input: bfloat16 [16384, 2048], P(('dp', 'sp'))
- shared_new: float32 [6, 2048], replicated
- shared_first_new: float32 [6, 2048], replicated
- shared_second_new: float32 [6, 2048], replicated
- split_new: float32 [8, 1792], P('tp')
- split_first_new: float32 [8, 1792], P('tp')
- split_second_new: float32 [8, 1792], P('tp')
- qkv_new: float32 [16, 128, 6144], P(('dp', 'sp'), None, 'tp')
- qkv_first_new: float32 [16, 128, 6144], P(('dp', 'sp'), None, 'tp')
- qkv_second_new: float32 [16, 128, 6144], P(('dp', 'sp'), None, 'tp')
- qkv_copy: bfloat16 [16, 128, 6144], P(('dp', 'sp'), None, 'tp')
- out_new: float32 [2048, 16, 128], P('tp', ('dp', 'sp'))
- out_first_new: float32 [2048, 16, 128], P('tp', ('dp', 'sp'))
- out_second_new: float32 [2048, 16, 128], P('tp', ('dp', 'sp'))
- out_copy: bfloat16 [2048, 16, 128], P('tp', ('dp', 'sp'))
- up_new: float32 [16, 128, 8192], P(('dp', 'sp'), None, 'tp')
- up_first_new: float32 [16, 128, 8192], P(('dp', 'sp'), None, 'tp')
- up_second_new: float32 [16, 128, 8192], P(('dp', 'sp'), None, 'tp')
- up_copy: bfloat16 [16, 128, 8192], P(('dp', 'sp'), None, 'tp')
- down_new: float32 [8192, 16, 128], P('tp', ('dp', 'sp'))
- down_first_new: float32 [8192, 16, 128], P('tp', ('dp', 'sp'))
- down_second_new: float32 [8192, 16, 128], P('tp', ('dp', 'sp'))
- down_copy: bfloat16 [8192, 16, 128], P('tp', ('dp', 'sp'))
The draws below stay inside these ranges and needn't reach their ends.
Inputs may be any that keep to these rules, and one draw needn't show every extreme that they name: `seq_lens`: each group holds either one sequence of 2048 tokens (second entry 0) or two of 1024; every draw has groups of both kinds. `owners`: each row is a permutation of the slots. `qkv_left`: each square matrix is orthogonal. `qkv_right`: each square matrix is orthogonal. `out_left`: each square matrix is orthogonal. `out_right`: each square matrix is orthogonal. `up_left`: each square matrix is orthogonal. `up_right`: each square matrix is orthogonal. `down_left`: each square matrix is orthogonal. `down_right`: each square matrix is orthogonal.
All inputs are finite; a program needn't handle non-finite values.
Results may differ from the reference program's by a relative error of at most 0.0065.
The reference program's roundings to bfloat16 on the way count: a program that leaves them out, or rounds other values in their place, can miss the bound.
Values may be sent and summed in bfloat16 or wider, within the bound.
No kernel may reach another device: no remote copies, remote signals or barrier semaphores. Data moves between devices by JAX's collectives and lax.ppermute only.
A program may use at most 256 MiB of HBM per device.

```python
import math
import jax
import jax.numpy as jnp
from jax import lax

D = 2048
H = 8
FF = 8192
HS = 256
SHORT = 1024
LONG = 2048
GROUP = 2048
TOKENS = 16384
OWNERS = 16
SPLIT = 1792
STEP = 5
N_DP = 8
N_SP = 2
N_TP = 8


def bit_parity(masked, extent):
    bit_total = jnp.zeros_like(masked)
    for shift_count in range(max(extent - 1, 1).bit_length()):
        bit_total = bit_total + jnp.bitwise_and(jnp.right_shift(masked, shift_count), 1)
    return jnp.bitwise_and(bit_total, 1)


def signed_hadamard(key, amount, extent):
    subkeys = jax.random.split(key, 4)
    row_order = jax.vmap(lambda subkey: jax.random.permutation(subkey, extent))(jax.random.split(subkeys[0], amount))
    col_order = jax.vmap(lambda subkey: jax.random.permutation(subkey, extent))(jax.random.split(subkeys[1], amount))
    row_signs = (2 * jax.random.randint(subkeys[2], (amount, extent), 0, 2) - 1).astype(jnp.float32)
    col_signs = (2 * jax.random.randint(subkeys[3], (amount, extent), 0, 2) - 1).astype(jnp.float32)
    parity = bit_parity(jnp.bitwise_and(row_order[:, :, None], col_order[:, None, :]), extent)
    entries = (1 - 2 * parity).astype(jnp.float32) / math.sqrt(extent)
    return entries * row_signs[:, :, None] * col_signs[:, None, :]


def rotation_three(key, amount):
    angles = jax.random.uniform(key, (amount, 3), minval=-math.pi, maxval=math.pi)
    cos_yaw = jnp.cos(angles[:, 0])
    sin_yaw = jnp.sin(angles[:, 0])
    cos_pitch = jnp.cos(angles[:, 1])
    sin_pitch = jnp.sin(angles[:, 1])
    cos_roll = jnp.cos(angles[:, 2])
    sin_roll = jnp.sin(angles[:, 2])
    matrix_rows = [[cos_yaw * cos_pitch, cos_yaw * sin_pitch * sin_roll - sin_yaw * cos_roll, cos_yaw * sin_pitch * cos_roll + sin_yaw * sin_roll], [sin_yaw * cos_pitch, sin_yaw * sin_pitch * sin_roll + cos_yaw * cos_roll, sin_yaw * sin_pitch * cos_roll - cos_yaw * sin_roll], [-sin_pitch, cos_pitch * sin_roll, cos_pitch * cos_roll]]
    return jnp.stack([jnp.stack(matrix_row, axis=-1) for matrix_row in matrix_rows], axis=-2)


def orthogonal(key, amount, extent):
    if extent % 3 == 0:
        reduced = extent // 3
        first_key, second_key = jax.random.split(key)
        hadamard = signed_hadamard(first_key, amount, reduced)
        rotation = rotation_three(second_key, amount)
        return (rotation[:, :, None, :, None] * hadamard[:, None, :, None, :]).reshape(amount, extent, extent)
    return signed_hadamard(key, amount, extent)


def basis_stack(key, extent):
    return orthogonal(key, OWNERS * N_TP, extent).reshape(OWNERS, N_TP, extent, extent)


def draw_seq_lens(key, part):
    key = jax.random.fold_in(key, 2)
    first_key, second_key = jax.random.split(key)
    kinds = jax.random.randint(first_key, (N_DP,), 0, 2)
    chosen = jax.random.permutation(second_key, N_DP)
    kinds = kinds.at[chosen[0]].set(1).at[chosen[1]].set(0)
    first_len = jnp.where(kinds == 1, LONG, SHORT)
    second_len = jnp.where(kinds == 1, 0, SHORT)
    return jnp.stack([first_len, second_len], axis=1).astype(jnp.int32)


def draw_shared_vec(key, part):
    key = jax.random.fold_in(key, 1)
    first_key, second_key = jax.random.split(key)
    spread = 0.4
    gains = 1.0 + jax.random.uniform(first_key, (6, D), minval=-spread, maxval=spread)
    shifts = jnp.clip(0.3 * jax.random.normal(second_key, (6, D)), -1.5, 1.5)
    row_index = jnp.arange(6)
    is_gain = (row_index % 2 == 0) & (row_index < 4)
    return jnp.where(is_gain[:, None], gains, shifts).astype(jnp.float32)


def draw_qkv_left(key, part):
    key = jax.random.fold_in(key, 11)
    return basis_stack(key, D // OWNERS)


def draw_qkv_right(key, part):
    key = jax.random.fold_in(key, 12)
    return basis_stack(key, 3 * D // N_TP)


def draw_out_left(key, part):
    key = jax.random.fold_in(key, 13)
    return basis_stack(key, D // N_TP)


def draw_out_right(key, part):
    key = jax.random.fold_in(key, 14)
    return basis_stack(key, D // OWNERS)


def draw_up_left(key, part):
    key = jax.random.fold_in(key, 15)
    return basis_stack(key, D // OWNERS)


def draw_up_right(key, part):
    key = jax.random.fold_in(key, 16)
    return basis_stack(key, FF // N_TP)


def draw_down_left(key, part):
    key = jax.random.fold_in(key, 17)
    return basis_stack(key, FF // N_TP)


def draw_down_right(key, part):
    key = jax.random.fold_in(key, 18)
    return basis_stack(key, D // OWNERS)


def block_levels(key, dims, pieces, least, top_value):
    loudness = 1.0
    for dim, shards_of in pieces:
        draws = jax.random.uniform(jax.random.fold_in(jax.random.fold_in(key, 6), dim), (shards_of,), jnp.float32, least / len(pieces), top_value / len(pieces))
        loudness = loudness * jnp.repeat(jnp.exp(draws), dims[dim] // shards_of).reshape((-1,) + (1,) * (len(dims) - 1 - dim))
    return loudness


def scatter_about(own_key, dims, deviation, limit, shards=(), kind=jnp.bfloat16):
    values = deviation * jax.random.normal(own_key, dims, jnp.float32)
    if shards:
        values = values * block_levels(own_key, dims, shards, -0.22, 0.18)
    return jnp.clip(values, -limit, limit).astype(kind)


def setup_inputs(seed: int = 0) -> dict:
    keys = jax.random.split(jax.random.key(seed), 31)
    return {
        "tokens": scatter_about(keys[0], (TOKENS, D), 1.0, 6.0, ((0, 16),)),
        "cotangent": scatter_about(keys[1], (TOKENS, D), 1.0, 6.0, ((0, 16),)),
        "seq_lens": draw_seq_lens(jax.random.fold_in(keys[30], 71), 0),
        "owners": jax.vmap(lambda own: jax.random.permutation(own, OWNERS))(jax.random.split(keys[3], 4)).reshape((4, OWNERS)).astype(jnp.int32),
        "shared_vec": draw_shared_vec(jax.random.fold_in(keys[30], 71), 0),
        "shared_first": scatter_about(keys[5], (6, D), (TOKENS ** 0.5), 768.0, (), jnp.float32),
        "shared_second": jnp.clip(jnp.exp(jax.random.uniform(keys[6], (6, D), jnp.float32, math.log(16384.0), math.log(65536.0))), 16384.0, 65536.0),
        "split_vec": scatter_about(keys[7], (N_TP, SPLIT), 0.05, 0.75, ((0, 8),), jnp.float32),
        "split_first": scatter_about(keys[8], (N_TP, SPLIT), (0.5 * TOKENS ** 0.5), 384.0, ((0, 8),), jnp.float32),
        "split_second": jnp.clip(jnp.exp(math.log(16384.0) - 1.3862944 * jax.random.uniform(keys[9], (N_TP, SPLIT), jnp.float32) ** block_levels(keys[9], (N_TP, SPLIT), ((0, 8),), -0.2, 0.2)), 4096.0, 16384.0),
        "qkv_master": scatter_about(keys[10], (OWNERS, D // OWNERS, 3 * D), D ** -0.5, 0.125, ((0, 16), (2, 8)), jnp.float32),
        "qkv_first": scatter_about(keys[11], (OWNERS, D // OWNERS, 3 * D), (2 * TOKENS ** 0.5), 1536.0, ((0, 16), (2, 8)), jnp.float32),
        "qkv_second": jnp.clip(jnp.exp(math.log(262144.0) - 1.3862944 * jax.random.uniform(keys[12], (OWNERS, D // OWNERS, 3 * D), jnp.float32) ** block_levels(keys[12], (OWNERS, D // OWNERS, 3 * D), ((0, 16), (2, 8)), -0.2, 0.2)), 65536.0, 262144.0),
        "qkv_left": draw_qkv_left(jax.random.fold_in(keys[30], 71), 0),
        "qkv_right": draw_qkv_right(jax.random.fold_in(keys[30], 71), 0),
        "out_master": scatter_about(keys[15], (D, OWNERS, D // OWNERS), (max(D // 128, 2)) ** -0.5, 1.5, ((0, 8), (1, 16)), jnp.float32),
        "out_first": scatter_about(keys[16], (D, OWNERS, D // OWNERS), (0.1 * TOKENS ** 0.5), 80.0, ((0, 8), (1, 16)), jnp.float32),
        "out_second": jnp.clip(jnp.exp(math.log(655.36) - 1.3862944 * jax.random.uniform(keys[17], (D, OWNERS, D // OWNERS), jnp.float32) ** block_levels(keys[17], (D, OWNERS, D // OWNERS), ((0, 8), (1, 16)), -0.2, 0.2)), 163.84, 655.36),
        "out_left": draw_out_left(jax.random.fold_in(keys[30], 71), 0),
        "out_right": draw_out_right(jax.random.fold_in(keys[30], 71), 0),
        "up_master": scatter_about(keys[20], (OWNERS, D // OWNERS, FF), D ** -0.5, 0.125, ((0, 16), (2, 8)), jnp.float32),
        "up_first": scatter_about(keys[21], (OWNERS, D // OWNERS, FF), (0.3 * TOKENS ** 0.5), 224.0, ((0, 16), (2, 8)), jnp.float32),
        "up_second": jnp.clip(jnp.exp(math.log(5898.24) - 1.3862944 * jax.random.uniform(keys[22], (OWNERS, D // OWNERS, FF), jnp.float32) ** block_levels(keys[22], (OWNERS, D // OWNERS, FF), ((0, 16), (2, 8)), -0.2, 0.2)), 1474.56, 5898.24),
        "up_left": draw_up_left(jax.random.fold_in(keys[30], 71), 0),
        "up_right": draw_up_right(jax.random.fold_in(keys[30], 71), 0),
        "down_master": scatter_about(keys[25], (FF, OWNERS, D // OWNERS), FF ** -0.5, 0.0625, ((0, 8), (1, 16)), jnp.float32),
        "down_first": scatter_about(keys[26], (FF, OWNERS, D // OWNERS), (0.6 * TOKENS ** 0.5), 448.0, ((0, 8), (1, 16)), jnp.float32),
        "down_second": jnp.clip(jnp.exp(math.log(23592.96) - 1.3862944 * jax.random.uniform(keys[27], (FF, OWNERS, D // OWNERS), jnp.float32) ** block_levels(keys[27], (FF, OWNERS, D // OWNERS), ((0, 8), (1, 16)), -0.2, 0.2)), 5898.24, 23592.96),
        "down_left": draw_down_left(jax.random.fold_in(keys[30], 71), 0),
        "down_right": draw_down_right(jax.random.fold_in(keys[30], 71), 0),
    }


ln_eps = 1e-05
adam_eps = 1e-08
beta_one = 0.5
beta_two = 0.5
rate_qkv = 0.01
rate_out = 0.05
rate_up = 0.01
rate_down = 0.005
rate_vector = 0.2
weight_decay = 0.01

@jax.custom_vjp
def low(v):
    return lax.optimization_barrier(v.astype(jnp.bfloat16)).astype(jnp.float32)

@jax.custom_vjp
def low_back(v):
    return v

def low_keep(v):
    return (low(v), None)

def low_pass(kept, grad):
    return (grad,)

def back_keep(v):
    return (v, None)

def back_low(kept, grad):
    return (low(grad),)
low.defvjp(low_keep, low_pass)
low_back.defvjp(back_keep, back_low)

def exact_dot(left_matrix, right_matrix):
    return jnp.dot(left_matrix, right_matrix, precision=lax.Precision.HIGHEST, preferred_element_type=jnp.float32)

def layer_norm(field, gain, shift):
    center = field - lax.optimization_barrier(jnp.mean(field, axis=-1, keepdims=True))
    spread = lax.optimization_barrier(jnp.mean(center * center, axis=-1, keepdims=True))
    return center * lax.rsqrt(spread + ln_eps) * gain + shift

def gelu_exact(field):
    return jax.nn.gelu(field, approximate=False)

def rotate(field, places, rot_dims):
    half_dims = rot_dims // 2
    frequency = 10000.0 ** (-2.0 * jnp.arange(half_dims, dtype=jnp.float32) / rot_dims)
    angles = places.astype(jnp.float32)[:, None] * frequency[None, :]
    cosine = jnp.cos(angles)[:, None, :]
    sine_part = jnp.sin(angles)[:, None, :]
    front = field[..., :half_dims]
    middle = field[..., half_dims:rot_dims]
    return jnp.concatenate([front * cosine - middle * sine_part, middle * cosine + front * sine_part, field[..., rot_dims:]], axis=-1)

def row_places(first_len, second_len, part_index, local_index, part_count):
    first_rows = first_len // part_count
    in_first = local_index < first_rows
    segment = jnp.where(in_first, 0, 1).astype(jnp.int32)
    position = jnp.where(in_first, part_index * first_rows + local_index, part_index * (second_len // part_count) + local_index - first_rows).astype(jnp.int32)
    return (segment, position)

def soap_block(gradient, weight, first_moment, second_moment, left_basis, right_basis, step_rate):
    turned = exact_dot(exact_dot(left_basis.T, gradient), right_basis)
    first_new = beta_one * first_moment + (1.0 - beta_one) * turned
    second_new = beta_two * second_moment + (1.0 - beta_two) * turned * turned
    direction = first_new / (1.0 - beta_one ** STEP) / (jnp.sqrt(second_new / (1.0 - beta_two ** STEP)) + adam_eps)
    returned = exact_dot(exact_dot(left_basis, direction), right_basis.T)
    return (weight * (1.0 - step_rate * weight_decay) - step_rate * returned, first_new, second_new)

def adam_vector(gradient, current, first_moment, second_moment):
    first_new = beta_one * first_moment + (1.0 - beta_one) * gradient
    second_new = beta_two * second_moment + (1.0 - beta_two) * gradient * gradient
    direction = first_new / (1.0 - beta_one ** STEP) / (jnp.sqrt(second_new / (1.0 - beta_two ** STEP)) + adam_eps)
    return (current - rate_vector * direction, first_new, second_new)

def row_owned(gradient, master, first_moment, second_moment, left_basis, right_basis, order, step_rate):
    group_count, block_rows, columns = master.shape
    width = columns // N_TP
    blocks = gradient.reshape(group_count, block_rows, N_TP, width)
    slotted = jnp.zeros_like(blocks).at[order].set(blocks)

    def arrange(field):
        return field.reshape(group_count, block_rows, N_TP, width).transpose(0, 2, 1, 3)

    def restore(field):
        return field.transpose(0, 2, 1, 3).reshape(group_count, block_rows, columns)

    def update(grad_block, weight, first_block, second_block, left_block, right_block):
        return soap_block(grad_block, weight, first_block, second_block, left_block, right_block, step_rate)
    results = jax.vmap(jax.vmap(update))(arrange(slotted), arrange(master), arrange(first_moment), arrange(second_moment), left_basis, right_basis)
    return (restore(results[0]), restore(results[1]), restore(results[2]))

def column_owned(gradient, master, first_moment, second_moment, left_basis, right_basis, order, step_rate):
    row_total, group_count, block_cols = master.shape
    height = row_total // N_TP
    blocks = gradient.reshape(N_TP, height, group_count, block_cols)
    slotted = jnp.zeros_like(blocks).at[:, :, order].set(blocks)

    def arrange(field):
        return field.reshape(N_TP, height, group_count, block_cols).transpose(2, 0, 1, 3)

    def restore(field):
        return field.transpose(1, 2, 0, 3).reshape(row_total, group_count, block_cols)

    def update(grad_block, weight, first_block, second_block, left_block, right_block):
        return soap_block(grad_block, weight, first_block, second_block, left_block, right_block, step_rate)
    results = jax.vmap(jax.vmap(update))(arrange(slotted), arrange(master), arrange(first_moment), arrange(second_moment), left_basis, right_basis)
    return (restore(results[0]), restore(results[1]), restore(results[2]))

def reference(tokens, cotangent, seq_lens, owners, shared_vec, shared_first, shared_second, split_vec, split_first, split_second, qkv_master, qkv_first, qkv_second, qkv_left, qkv_right, out_master, out_first, out_second, out_left, out_right, up_master, up_first, up_second, up_left, up_right, down_master, down_first, down_second, down_left, down_right):
    group_rows = GROUP // N_SP
    qkv_cols = 3 * D // N_TP
    local_all = jnp.arange(GROUP, dtype=jnp.int32)
    segment, position = row_places(seq_lens[:, 0:1], seq_lens[:, 1:2], (local_all // group_rows)[None, :], (local_all % group_rows)[None, :], N_SP)
    flat_position = position.reshape(TOKENS)
    scale = HS ** (-0.5)
    segment_heads = jnp.repeat(segment, H, axis=0)
    position_heads = jnp.repeat(position, H, axis=0)

    def head_attend(items):
        query, key_part, value_part, head_segment, head_position = items
        scores = low_back(exact_dot(query, key_part.T)) * scale
        visible = (head_segment[:, None] == head_segment[None, :]) & (head_position[None, :] <= head_position[:, None])
        scores = jnp.where(visible, scores, -1e+30)
        probability = low(jax.nn.softmax(scores, axis=-1))
        return low_back(low(exact_dot(probability, value_part)))

    def arrange(field):
        return field.reshape(N_DP, GROUP, H, HS).transpose(0, 2, 1, 3).reshape(N_DP * H, GROUP, HS)

    def forward(field, w_qkv, w_out, w_up, w_down, shared, b_qkv, b_up):
        h_one = low(layer_norm(field, shared[0], shared[1]))
        h_two = low(layer_norm(field, shared[2], shared[3]))
        qkv = low_back(exact_dot(h_one, low(w_qkv)) + b_qkv).reshape(TOKENS, H, 3, HS)
        query = low(rotate(qkv[:, :, 0], flat_position, HS // 4))
        key_all = low(rotate(qkv[:, :, 1], flat_position, HS // 4))
        value_all = low(qkv[:, :, 2])
        heads_out = lax.map(jax.checkpoint(head_attend), (arrange(query), arrange(key_all), arrange(value_all), segment_heads, position_heads))
        attended = heads_out.reshape(N_DP, H, GROUP, HS).transpose(0, 2, 1, 3).reshape(TOKENS, D)
        attention = exact_dot(attended, low(w_out)) + shared[4]
        hidden = low(gelu_exact(low_back(exact_dot(h_two, low(w_up)) + b_up)))
        feed = exact_dot(hidden, low(w_down)) + shared[5]
        return field + attention + feed
    w_qkv = jnp.take(qkv_master, owners[0], axis=0).reshape(D, 3 * D)
    w_out = jnp.take(out_master, owners[1], axis=1).reshape(D, D)
    w_up = jnp.take(up_master, owners[2], axis=0).reshape(D, FF)
    w_down = jnp.take(down_master, owners[3], axis=1).reshape(FF, D)
    b_qkv = split_vec[:, :qkv_cols].reshape(3 * D)
    b_up = split_vec[:, qkv_cols:].reshape(FF)
    field = tokens.astype(jnp.float32)
    result, pullback = jax.vjp(forward, field, w_qkv, w_out, w_up, w_down, shared_vec, b_qkv, b_up)
    grads = pullback(cotangent.astype(jnp.float32))
    grad_field, grad_qkv, grad_out, grad_up, grad_down, grad_shared, grad_bqkv, grad_bup = grads
    split_grad = jnp.concatenate([grad_bqkv.reshape(N_TP, qkv_cols), grad_bup.reshape(N_TP, FF // N_TP)], axis=1)
    shared_new = adam_vector(grad_shared, shared_vec, shared_first, shared_second)
    split_new = adam_vector(split_grad, split_vec, split_first, split_second)
    qkv_new = row_owned(grad_qkv, qkv_master, qkv_first, qkv_second, qkv_left, qkv_right, owners[0], rate_qkv)
    out_new = column_owned(grad_out, out_master, out_first, out_second, out_left, out_right, owners[1], rate_out)
    up_new = row_owned(grad_up, up_master, up_first, up_second, up_left, up_right, owners[2], rate_up)
    down_new = column_owned(grad_down, down_master, down_first, down_second, down_left, down_right, owners[3], rate_down)
    return (result.astype(jnp.bfloat16), grad_field.astype(jnp.bfloat16), shared_new[0], shared_new[1], shared_new[2], split_new[0], split_new[1], split_new[2], qkv_new[0], qkv_new[1], qkv_new[2], qkv_new[0].astype(jnp.bfloat16), out_new[0], out_new[1], out_new[2], out_new[0].astype(jnp.bfloat16), up_new[0], up_new[1], up_new[2], up_new[0].astype(jnp.bfloat16), down_new[0], down_new[1], down_new[2], down_new[0].astype(jnp.bfloat16))
```

```python
import jax
import jax.numpy as jnp
from jax import lax
from jax.experimental import pallas as pl
from jax.experimental.pallas import tpu as pltpu
from jax.sharding import Mesh, PartitionSpec as P

D = 2048
H = 8
STEP = 5


ln_eps = 1e-05
adam_eps = 1e-08
beta_one = 0.5
beta_two = 0.5
rate_qkv = 0.01
rate_out = 0.05
rate_up = 0.01
rate_down = 0.005
rate_vector = 0.2
weight_decay = 0.01


def exact_dot(left_matrix, right_matrix):
    return jnp.dot(
        left_matrix,
        right_matrix,
        precision=lax.Precision.HIGHEST,
        preferred_element_type=jnp.float32,
    )


def contract_rows(left_matrix, right_matrix):
    return lax.dot_general(
        left_matrix, right_matrix, (((0,), (0,)), ((), ())), preferred_element_type=jnp.float32
    )


def contract_cols(left_matrix, right_matrix):
    return lax.dot_general(
        left_matrix, right_matrix, (((1,), (1,)), ((), ())), preferred_element_type=jnp.float32
    )


def layer_norm(field, gain, shift):
    center = field - jnp.mean(field, axis=-1, keepdims=True)
    spread = jnp.mean(center * center, axis=-1, keepdims=True)
    return center * lax.rsqrt(spread + ln_eps) * gain + shift


def gelu_exact(field):
    return jax.nn.gelu(field, approximate=False)


def rotate(field, places, rot_dims):
    half_dims = rot_dims // 2
    frequency = 10000.0 ** (-2.0 * jnp.arange(half_dims, dtype=jnp.float32) / rot_dims)
    angles = places.astype(jnp.float32)[:, None] * frequency[None, :]
    cosine = jnp.cos(angles)[:, None, :]
    sine_part = jnp.sin(angles)[:, None, :]
    front = field[..., :half_dims]
    middle = field[..., half_dims:rot_dims]
    return jnp.concatenate(
        [
            front * cosine - middle * sine_part,
            middle * cosine + front * sine_part,
            field[..., rot_dims:],
        ],
        axis=-1,
    )


def row_places(first_len, second_len, part_index, local_index, part_count):
    first_rows = first_len // part_count
    in_first = local_index < first_rows
    segment = jnp.where(in_first, 0, 1).astype(jnp.int32)
    position = jnp.where(
        in_first,
        part_index * first_rows + local_index,
        part_index * (second_len // part_count) + local_index - first_rows,
    )
    return (segment, position)


def soap_block(gradient, weight, first_moment, second_moment, left_basis, right_basis, step_rate):
    turned = exact_dot(exact_dot(left_basis.T, gradient), right_basis)
    first_new = beta_one * first_moment + (1.0 - beta_one) * turned
    second_new = beta_two * second_moment + (1.0 - beta_two) * turned * turned
    direction = (
        first_new
        / (1.0 - beta_one**STEP)
        / (jnp.sqrt(second_new / (1.0 - beta_two**STEP)) + adam_eps)
    )
    returned = exact_dot(exact_dot(left_basis, direction), right_basis.T)
    return (weight * (1.0 - step_rate * weight_decay) - step_rate * returned, first_new, second_new)


def adam_vector(gradient, current, first_moment, second_moment):
    first_new = beta_one * first_moment + (1.0 - beta_one) * gradient
    second_new = beta_two * second_moment + (1.0 - beta_two) * gradient * gradient
    direction = (
        first_new
        / (1.0 - beta_one**STEP)
        / (jnp.sqrt(second_new / (1.0 - beta_two**STEP)) + adam_eps)
    )
    return (current - rate_vector * direction, first_new, second_new)


UP = [(i, (i + 1) % 4) for i in range(4)]
DOWN = [(i, (i + 3) % 4) for i in range(4)]
PAIR = [(0, 1), (1, 0)]
bf16 = jnp.bfloat16
f32 = jnp.float32


def relative_slots():
    y, c, s = lax.axis_index("y"), lax.axis_index("c"), lax.axis_index("s")
    r = jnp.arange(16, dtype=jnp.int32)
    core = c ^ (r // 8)
    row = (y + (r // 2) % 4) % 4
    part = s ^ (r % 2)
    return (row * 2 + core) * 2 + part


def place_blocks(places, sources, plan, out_shape, columns):
    block = sources[0].shape[1:]

    def kernel(place_ref, *refs):
        ins, out, hold, in_sems, out_sems = refs[:-4], refs[-4], refs[-3], refs[-2], refs[-1]
        inward, outward = [], []
        for k, (which, part) in enumerate(plan):
            if columns:
                start = pl.multiple_of(place_ref[k] * block[1], block[1])
                target = out.at[:, pl.ds(start, block[1])]
            else:
                start = pl.multiple_of(place_ref[k] * block[0], block[0])
                target = out.at[pl.ds(start, block[0])]
            inward.append(pltpu.make_async_copy(ins[which].at[part], hold.at[k], in_sems.at[k]))
            outward.append(pltpu.make_async_copy(hold.at[k], target, out_sems.at[k]))
        for copy in inward:
            copy.start()
        for first, second in zip(inward, outward):
            first.wait()
            second.start()
        for copy in outward:
            copy.wait()

    return pl.pallas_call(
        kernel,
        out_shape=jax.ShapeDtypeStruct(out_shape, sources[0].dtype),
        in_specs=[pl.BlockSpec(memory_space=pltpu.SMEM)]
        + [pl.BlockSpec(memory_space=pl.ANY)] * len(sources),
        out_specs=pl.BlockSpec(memory_space=pl.ANY),
        scratch_shapes=[
            pltpu.VMEM((len(plan), *block), sources[0].dtype),
            pltpu.SemaphoreType.DMA((len(plan),)),
            pltpu.SemaphoreType.DMA((len(plan),)),
        ],
        compiler_params=pltpu.CompilerParams(vmem_limit_bytes=32 * 2**20),
    )(places, *sources)


def pick_blocks(places, field, out_shape, columns):
    amount = out_shape[0]
    block = out_shape[1:]

    def kernel(place_ref, field_ref, out, hold, in_sems, out_sems):
        inward, outward = [], []
        for k in range(amount):
            if columns:
                start = pl.multiple_of(place_ref[k] * block[1], block[1])
                origin = field_ref.at[:, pl.ds(start, block[1])]
            else:
                start = pl.multiple_of(place_ref[k] * block[0], block[0])
                origin = field_ref.at[pl.ds(start, block[0])]
            inward.append(pltpu.make_async_copy(origin, hold.at[k], in_sems.at[k]))
            outward.append(pltpu.make_async_copy(hold.at[k], out.at[k], out_sems.at[k]))
        for copy in inward:
            copy.start()
        for first, second in zip(inward, outward):
            first.wait()
            second.start()
        for copy in outward:
            copy.wait()

    return pl.pallas_call(
        kernel,
        out_shape=jax.ShapeDtypeStruct(out_shape, field.dtype),
        in_specs=[pl.BlockSpec(memory_space=pltpu.SMEM), pl.BlockSpec(memory_space=pl.ANY)],
        out_specs=pl.BlockSpec(memory_space=pl.ANY),
        scratch_shapes=[
            pltpu.VMEM(out_shape, field.dtype),
            pltpu.SemaphoreType.DMA((amount,)),
            pltpu.SemaphoreType.DMA((amount,)),
        ],
        compiler_params=pltpu.CompilerParams(vmem_limit_bytes=32 * 2**20),
    )(places, field)


def fetch(block):
    pair = jnp.concatenate([block, lax.ppermute(block, "s", PAIR)], axis=0)
    before = lax.ppermute(pair, "y", UP)
    after = lax.ppermute(pair, "y", DOWN)
    far_a = lax.ppermute(before[0:1], "y", UP)
    far_b = lax.ppermute(after[1:2], "y", DOWN)
    half = jnp.concatenate([pair, after, far_a, far_b, before], axis=0)
    other = lax.ppermute(half, "c", PAIR)
    return [half, other]


FETCH_PLAN = [(k // 8, k % 8) for k in range(16)]


def deliver(blocks):
    sibling = lax.ppermute(blocks[8:], "c", PAIR)

    def both(low, high):
        return blocks[low:high].astype(f32) + sibling[low:high].astype(f32)

    far_a = lax.ppermute(both(4, 5).astype(bf16), "y", UP)
    far_b = lax.ppermute(both(5, 6).astype(bf16), "y", DOWN)
    to_next = jnp.concatenate([both(2, 3) + far_a.astype(f32), both(3, 4)], axis=0).astype(bf16)
    to_prev = jnp.concatenate([both(6, 7), both(7, 8) + far_b.astype(f32)], axis=0).astype(bf16)
    from_prev = lax.ppermute(to_next, "y", UP)
    from_next = lax.ppermute(to_prev, "y", DOWN)
    total = both(0, 2) + from_prev.astype(f32) + from_next.astype(f32)
    partner = lax.ppermute(total[1:2].astype(bf16), "s", PAIR)
    return total[0] + partner[0].astype(f32)


def tp_sum_rows(partial):
    x, z = lax.axis_index("x"), lax.axis_index("z")

    def rows(offset, low, size):
        start = ((x + offset) % 4) * 256 + low
        return lax.dynamic_slice_in_dim(partial, start, size, axis=0).astype(f32)

    far_a = lax.ppermute(rows(2, 0, 128).astype(bf16), "x", UP)
    far_b = lax.ppermute(rows(2, 128, 128).astype(bf16), "x", DOWN)
    to_next = jnp.concatenate([rows(1, 0, 128) + far_a.astype(f32), rows(1, 128, 128)], axis=0).astype(bf16)
    to_prev = jnp.concatenate([rows(3, 0, 128), rows(3, 128, 128) + far_b.astype(f32)], axis=0).astype(bf16)
    from_prev = lax.ppermute(to_next, "x", UP)
    from_next = lax.ppermute(to_prev, "x", DOWN)

    def total(start):
        own = lax.dynamic_slice_in_dim(partial, x * 256 + start, 128, axis=0).astype(f32)
        one = lax.dynamic_slice_in_dim(from_prev, start, 128, axis=0).astype(f32)
        two = lax.dynamic_slice_in_dim(from_next, start, 128, axis=0).astype(f32)
        return own + one + two

    partner = lax.ppermute(total((1 - z) * 128).astype(bf16), "z", PAIR)
    return total(z * 128) + partner.astype(f32)


def tp_gather_rows(rows):
    x, z = lax.axis_index("x"), lax.axis_index("z")
    partner = lax.ppermute(rows, "z", PAIR)
    low = jnp.where(z == 0, rows, partner)
    high = jnp.where(z == 0, partner, rows)
    pair = jnp.stack([low, high])
    before = lax.ppermute(pair, "x", UP)
    after = lax.ppermute(pair, "x", DOWN)
    far_a = lax.ppermute(before[0:1], "x", UP)
    far_b = lax.ppermute(after[1:2], "x", DOWN)
    steps = jnp.array([0, 0, 1, 1, 2, 2, 3, 3], jnp.int32)
    places = ((x + steps) % 4) * 2 + jnp.arange(8, dtype=jnp.int32) % 2
    plan = [(0, 0), (0, 1), (1, 0), (1, 1), (2, 0), (3, 0), (4, 0), (4, 1)]
    return place_blocks(
        places, [pair, after, far_a, far_b, before], plan, (1024, rows.shape[1]), False
    )


def exchange_add(vector, axis, order):
    return vector + lax.ppermute(vector, axis, order)


def per_device(
    tokens,
    cotangent,
    seq_lens,
    owners,
    shared_vec,
    shared_first,
    shared_second,
    split_vec,
    split_first,
    split_second,
    qkv_master,
    qkv_first,
    qkv_second,
    qkv_left,
    qkv_right,
    out_master,
    out_first,
    out_second,
    out_left,
    out_right,
    up_master,
    up_first,
    up_second,
    up_left,
    up_right,
    down_master,
    down_first,
    down_second,
    down_left,
    down_right,
):
    row_count = tokens.shape[0]
    head_size = D // H
    qkv_cols = qkv_master.shape[2]
    sp_rank = lax.axis_index("s")
    x, z = lax.axis_index("x"), lax.axis_index("z")
    tp_rank = x * 2 + z
    scale = head_size ** (-0.5)
    rot_dims = head_size // 4
    slots = relative_slots()
    block_ids = jnp.arange(16, dtype=jnp.int32)
    places = jnp.sum(
        jnp.where(owners[:, None, :] == slots[None, :, None], block_ids[None, None, :], 0), axis=2
    )
    qkv_low = qkv_master.astype(bf16)
    out_low = out_master.astype(bf16).reshape(1, 256, 128)
    up_low = up_master.astype(bf16)
    down_low = down_master.astype(bf16).reshape(1, 1024, 128)
    w_qkv = place_blocks(places[0], fetch(qkv_low), FETCH_PLAN, (2048, 768), False)
    w_out = place_blocks(places[1], fetch(out_low), FETCH_PLAN, (256, 2048), True)
    w_up = place_blocks(places[2], fetch(up_low), FETCH_PLAN, (2048, 1024), False)
    w_down = place_blocks(places[3], fetch(down_low), FETCH_PLAN, (1024, 2048), True)
    field = tokens.astype(f32)
    center = field - jnp.mean(field, axis=-1, keepdims=True)
    inverse_std = lax.rsqrt(jnp.mean(center * center, axis=-1, keepdims=True) + ln_eps)
    unit = center * inverse_std
    h_one = (unit * shared_vec[0] + shared_vec[1]).astype(bf16)
    h_two = (unit * shared_vec[2] + shared_vec[3]).astype(bf16)
    b_qkv = split_vec[0, :qkv_cols]
    b_up = split_vec[0, qkv_cols:]
    qkv_raw = jnp.dot(h_one, w_qkv, preferred_element_type=f32) + b_qkv
    local_index = jnp.arange(row_count, dtype=jnp.int32)
    query_seg, query_pos = row_places(seq_lens[0, 0], seq_lens[0, 1], sp_rank, local_index, 2)
    far_seg, far_pos = row_places(seq_lens[0, 0], seq_lens[0, 1], 0, local_index, 2)
    far_seg = jnp.where(sp_rank == 1, far_seg, 2)

    def turned(values_in):
        return rotate(values_in[:, None, :], query_pos, rot_dims)[:, 0]

    query_raw = qkv_raw[:, :256]
    key_raw = qkv_raw[:, 256:512]
    query_low = turned(query_raw).astype(bf16)
    key_low = turned(key_raw).astype(bf16)
    value_low = qkv_raw[:, 512:].astype(bf16)
    far_kv = lax.ppermute(jnp.stack([key_low, value_low]), "s", [(0, 1)])
    key_all = jnp.concatenate([key_low, far_kv[0]], axis=0)
    value_all = jnp.concatenate([value_low, far_kv[1]], axis=0)
    key_seg = jnp.concatenate([query_seg, far_seg])
    key_pos = jnp.concatenate([query_pos, far_pos])
    visible = (query_seg[:, None] == key_seg[None, :]) & (key_pos[None, :] <= query_pos[:, None])
    scores = contract_cols(query_low, key_all) * scale
    scores = jnp.where(visible, scores, -1e30)
    maximum = jnp.max(scores, axis=-1, keepdims=True)
    exponent = jnp.exp(scores - maximum)
    denominator = jnp.sum(exponent, axis=-1, keepdims=True)
    probability = exponent / denominator
    prob_low = probability.astype(bf16)
    attended_low = jnp.dot(prob_low, value_all, preferred_element_type=f32).astype(bf16)
    grad_attended = contract_cols(cotangent, w_out).astype(bf16)
    grad_probs = contract_cols(grad_attended, value_all)
    inner = jnp.sum(grad_probs * probability, axis=-1, keepdims=True)
    grad_scores = (probability * (grad_probs - inner) * scale).astype(bf16)
    grad_query = jnp.dot(grad_scores, key_all, preferred_element_type=f32)
    key_sum = contract_rows(grad_scores, query_low)
    value_sum = contract_rows(prob_low, grad_attended)
    far_grads = lax.ppermute(
        jnp.stack([key_sum[row_count:], value_sum[row_count:]]).astype(bf16), "s", [(1, 0)]
    ).astype(f32)
    grad_key = key_sum[:row_count] + far_grads[0]
    grad_value = value_sum[:row_count] + far_grads[1]
    query_back = jax.vjp(turned, query_raw)[1]
    key_back = jax.vjp(turned, key_raw)[1]
    grad_qkv = jnp.concatenate(
        [query_back(grad_query)[0], key_back(grad_key)[0], grad_value], axis=1
    ).astype(bf16)

    pre_act = jnp.dot(h_two, w_up, preferred_element_type=f32) + b_up
    hidden_low = gelu_exact(pre_act).astype(bf16)
    partial_out = (
        jnp.dot(attended_low, w_out, preferred_element_type=f32)
        + jnp.dot(hidden_low, w_down, preferred_element_type=f32)
    ).astype(bf16)
    own_start = tp_rank * 128

    def own(values_in):
        return lax.dynamic_slice_in_dim(values_in, own_start, 128, axis=0)

    branches = tp_sum_rows(partial_out)
    output = tp_gather_rows(
        (own(tokens).astype(f32) + branches + shared_vec[4] + shared_vec[5]).astype(bf16)
    )
    grad_hidden = contract_cols(cotangent, w_down)
    gelu_back = jax.vjp(gelu_exact, pre_act)[1]
    grad_pre = gelu_back(grad_hidden)[0].astype(bf16)
    grad_h_two = contract_cols(grad_pre, w_up)
    grad_h_one = contract_cols(grad_qkv, w_qkv)
    grad_unit = (grad_h_one * shared_vec[0] + grad_h_two * shared_vec[2]).astype(bf16)
    own_grad = tp_sum_rows(grad_unit)
    own_field = own(tokens).astype(f32)
    own_center = own_field - jnp.mean(own_field, axis=-1, keepdims=True)
    own_inverse = lax.rsqrt(jnp.mean(own_center * own_center, axis=-1, keepdims=True) + ln_eps)
    own_unit = own_center * own_inverse
    grad_x = (
        own_grad
        - jnp.mean(own_grad, axis=-1, keepdims=True)
        - own_unit * jnp.mean(own_grad * own_unit, axis=-1, keepdims=True)
    ) * own_inverse
    grad_input = tp_gather_rows((own(cotangent).astype(f32) + grad_x).astype(bf16))

    bias_share = jnp.sum(cotangent.astype(f32), axis=0) * 0.125
    shared_part = jnp.stack(
        [
            jnp.sum(grad_h_one * unit, axis=0),
            jnp.sum(grad_h_one, axis=0),
            jnp.sum(grad_h_two * unit, axis=0),
            jnp.sum(grad_h_two, axis=0),
            bias_share,
        ]
    )
    split_part = jnp.concatenate(
        [jnp.sum(grad_qkv.astype(f32), axis=0), jnp.sum(grad_pre.astype(f32), axis=0)]
    )
    sums = jnp.concatenate([shared_part.reshape(80, 128), split_part.reshape(14, 128)], axis=0)
    sums = exchange_add(sums, "c", PAIR)
    sums = exchange_add(sums, "s", PAIR)
    sums = exchange_add(sums, "y", [(i, i ^ 1) for i in range(4)])
    sums = exchange_add(sums, "y", [(i, i ^ 2) for i in range(4)])
    split_grad = sums[80:].reshape(1, 1792)
    shared_sum = exchange_add(sums[:80], "z", PAIR)
    shared_sum = exchange_add(shared_sum, "x", [(i, i ^ 1) for i in range(4)])
    shared_sum = exchange_add(shared_sum, "x", [(i, i ^ 2) for i in range(4)])
    shared_sum = shared_sum.reshape(5, 2048)
    shared_grad = jnp.concatenate([shared_sum, shared_sum[4:5]], axis=0)

    grad_out_w = contract_rows(attended_low, cotangent).astype(bf16)
    grad_down_w = contract_rows(hidden_low, cotangent).astype(bf16)
    grad_up_w = contract_rows(h_two, grad_pre).astype(bf16)
    grad_qkv_w = contract_rows(h_one, grad_qkv).astype(bf16)
    sum_qkv = deliver(pick_blocks(places[0], grad_qkv_w, (16, 128, 768), False))
    sum_out = deliver(pick_blocks(places[1], grad_out_w, (16, 256, 128), True))
    sum_up = deliver(pick_blocks(places[2], grad_up_w, (16, 128, 1024), False))
    sum_down = deliver(pick_blocks(places[3], grad_down_w, (16, 1024, 128), True))
    new_qkv = soap_block(
        sum_qkv,
        qkv_master[0],
        qkv_first[0],
        qkv_second[0],
        qkv_left[0, 0],
        qkv_right[0, 0],
        rate_qkv,
    )
    new_out = soap_block(
        sum_out,
        out_master[:, 0],
        out_first[:, 0],
        out_second[:, 0],
        out_left[0, 0],
        out_right[0, 0],
        rate_out,
    )
    new_up = soap_block(
        sum_up, up_master[0], up_first[0], up_second[0], up_left[0, 0], up_right[0, 0], rate_up
    )
    new_down = soap_block(
        sum_down,
        down_master[:, 0],
        down_first[:, 0],
        down_second[:, 0],
        down_left[0, 0],
        down_right[0, 0],
        rate_down,
    )
    new_shared = adam_vector(shared_grad, shared_vec, shared_first, shared_second)
    new_split = adam_vector(split_grad, split_vec, split_first, split_second)
    return (
        output,
        grad_input,
        new_shared[0],
        new_shared[1],
        new_shared[2],
        new_split[0],
        new_split[1],
        new_split[2],
        new_qkv[0][None],
        new_qkv[1][None],
        new_qkv[2][None],
        new_qkv[0][None].astype(bf16),
        new_out[0][:, None],
        new_out[1][:, None],
        new_out[2][:, None],
        new_out[0][:, None].astype(bf16),
        new_up[0][None],
        new_up[1][None],
        new_up[2][None],
        new_up[0][None].astype(bf16),
        new_down[0][:, None],
        new_down[1][:, None],
        new_down[2][:, None],
        new_down[0][:, None].astype(bf16),
    )


def solution(mesh):
    in_specs = (
        P(("y", "c", "s"), None),
        P(("y", "c", "s"), None),
        P(("y", "c"), None),
        P(),
        P(),
        P(),
        P(),
        P(("x", "z"), None),
        P(("x", "z"), None),
        P(("x", "z"), None),
        P(("y", "c", "s"), None, ("x", "z")),
        P(("y", "c", "s"), None, ("x", "z")),
        P(("y", "c", "s"), None, ("x", "z")),
        P(("y", "c", "s"), ("x", "z"), None, None),
        P(("y", "c", "s"), ("x", "z"), None, None),
        P(("x", "z"), ("y", "c", "s"), None),
        P(("x", "z"), ("y", "c", "s"), None),
        P(("x", "z"), ("y", "c", "s"), None),
        P(("y", "c", "s"), ("x", "z"), None, None),
        P(("y", "c", "s"), ("x", "z"), None, None),
        P(("y", "c", "s"), None, ("x", "z")),
        P(("y", "c", "s"), None, ("x", "z")),
        P(("y", "c", "s"), None, ("x", "z")),
        P(("y", "c", "s"), ("x", "z"), None, None),
        P(("y", "c", "s"), ("x", "z"), None, None),
        P(("x", "z"), ("y", "c", "s"), None),
        P(("x", "z"), ("y", "c", "s"), None),
        P(("x", "z"), ("y", "c", "s"), None),
        P(("y", "c", "s"), ("x", "z"), None, None),
        P(("y", "c", "s"), ("x", "z"), None, None),
    )
    out_specs = (
        P(("y", "c", "s"), None),
        P(("y", "c", "s"), None),
        P(),
        P(),
        P(),
        P(("x", "z"), None),
        P(("x", "z"), None),
        P(("x", "z"), None),
        P(("y", "c", "s"), None, ("x", "z")),
        P(("y", "c", "s"), None, ("x", "z")),
        P(("y", "c", "s"), None, ("x", "z")),
        P(("y", "c", "s"), None, ("x", "z")),
        P(("x", "z"), ("y", "c", "s"), None),
        P(("x", "z"), ("y", "c", "s"), None),
        P(("x", "z"), ("y", "c", "s"), None),
        P(("x", "z"), ("y", "c", "s"), None),
        P(("y", "c", "s"), None, ("x", "z")),
        P(("y", "c", "s"), None, ("x", "z")),
        P(("y", "c", "s"), None, ("x", "z")),
        P(("y", "c", "s"), None, ("x", "z")),
        P(("x", "z"), ("y", "c", "s"), None),
        P(("x", "z"), ("y", "c", "s"), None),
        P(("x", "z"), ("y", "c", "s"), None),
        P(("x", "z"), ("y", "c", "s"), None),
    )
    fine = Mesh(mesh.devices.reshape(4, 2, 2, 4, 2), ("y", "c", "s", "x", "z"))
    return jax.shard_map(
        per_device, mesh=fine, in_specs=in_specs, out_specs=out_specs, check_vma=False
    )
```

```python
import jax
import jax.numpy as jnp
from jax import lax
from jax.experimental import pallas as pl
from jax.experimental.pallas import tpu as pltpu
from jax.sharding import Mesh, PartitionSpec as P

D = 2048
H = 8
STEP = 5


ln_eps = 1e-05
adam_eps = 1e-08
beta_one = 0.5
beta_two = 0.5
rate_qkv = 0.01
rate_out = 0.05
rate_up = 0.01
rate_down = 0.005
rate_vector = 0.2
weight_decay = 0.01


def exact_dot(left_matrix, right_matrix):
    return jnp.dot(
        left_matrix,
        right_matrix,
        precision=lax.Precision.HIGH,
        preferred_element_type=jnp.float32,
    )


def contract_rows(left_matrix, right_matrix):
    return lax.dot_general(
        left_matrix, right_matrix, (((0,), (0,)), ((), ())), preferred_element_type=jnp.float32
    )


def contract_cols(left_matrix, right_matrix):
    return lax.dot_general(
        left_matrix, right_matrix, (((1,), (1,)), ((), ())), preferred_element_type=jnp.float32
    )


def layer_norm(field, gain, shift):
    center = field - jnp.mean(field, axis=-1, keepdims=True)
    spread = jnp.mean(center * center, axis=-1, keepdims=True)
    return center * lax.rsqrt(spread + ln_eps) * gain + shift


def gelu_exact(field):
    return jax.nn.gelu(field, approximate=False)


def rotate(field, places, rot_dims):
    half_dims = rot_dims // 2
    frequency = 10000.0 ** (-2.0 * jnp.arange(half_dims, dtype=jnp.float32) / rot_dims)
    angles = places.astype(jnp.float32)[:, None] * frequency[None, :]
    cosine = jnp.cos(angles)[:, None, :]
    sine_part = jnp.sin(angles)[:, None, :]
    front = field[..., :half_dims]
    middle = field[..., half_dims:rot_dims]
    return jnp.concatenate(
        [
            front * cosine - middle * sine_part,
            middle * cosine + front * sine_part,
            field[..., rot_dims:],
        ],
        axis=-1,
    )


def row_places(first_len, second_len, part_index, local_index, part_count):
    first_rows = first_len // part_count
    in_first = local_index < first_rows
    segment = jnp.where(in_first, 0, 1).astype(jnp.int32)
    position = jnp.where(
        in_first,
        part_index * first_rows + local_index,
        part_index * (second_len // part_count) + local_index - first_rows,
    )
    return (segment, position)


def soap_block(gradient, weight, first_moment, second_moment, left_basis, right_basis, step_rate):
    turned = exact_dot(exact_dot(left_basis.T, gradient), right_basis)
    first_new = beta_one * first_moment + (1.0 - beta_one) * turned
    second_new = beta_two * second_moment + (1.0 - beta_two) * turned * turned
    direction = (
        first_new
        / (1.0 - beta_one**STEP)
        / (jnp.sqrt(second_new / (1.0 - beta_two**STEP)) + adam_eps)
    )
    returned = exact_dot(exact_dot(left_basis, direction), right_basis.T)
    return (weight * (1.0 - step_rate * weight_decay) - step_rate * returned, first_new, second_new)


def adam_vector(gradient, current, first_moment, second_moment):
    first_new = beta_one * first_moment + (1.0 - beta_one) * gradient
    second_new = beta_two * second_moment + (1.0 - beta_two) * gradient * gradient
    direction = (
        first_new
        / (1.0 - beta_one**STEP)
        / (jnp.sqrt(second_new / (1.0 - beta_two**STEP)) + adam_eps)
    )
    return (current - rate_vector * direction, first_new, second_new)


UP = [(i, (i + 1) % 4) for i in range(4)]
DOWN = [(i, (i + 3) % 4) for i in range(4)]
PAIR = [(0, 1), (1, 0)]
GROUP_AXES = ("y", "c", "s")
bf16 = jnp.bfloat16
f32 = jnp.float32
ROWS = 1024
TILE = 256
ANY = pl.BlockSpec(memory_space=pl.ANY)
SCALARS = pl.BlockSpec(memory_space=pltpu.SMEM)
NN = (((1,), (0,)), ((), ()))
NT = (((1,), (1,)), ((), ()))
TN = (((0,), (0,)), ((), ()))


def mxu(left_matrix, right_matrix, dims):
    return lax.dot_general(left_matrix, right_matrix, dims, preferred_element_type=f32)


def wide(values):
    return values.astype(f32)


def low(values):
    return values.astype(bf16)


def struct(shape, dtype):
    return jax.ShapeDtypeStruct(shape, dtype)


def tiled(rows, columns):
    return pl.BlockSpec((rows, columns), lambda i: (i, 0))


def whole(*shape):
    return pl.BlockSpec(shape, lambda i: (0,) * len(shape))


def run(kernel, steps, ins, in_specs, outs, out_specs, scratch, flops, moved):
    return pl.pallas_call(
        kernel,
        name=kernel.__name__,
        grid=(steps,),
        in_specs=in_specs,
        out_specs=out_specs,
        out_shape=outs,
        scratch_shapes=scratch,
        compiler_params=pltpu.CompilerParams(vmem_limit_bytes=60 * 2**20),
        cost_estimate=pl.CostEstimate(flops=flops, bytes_accessed=moved, transcendentals=0),
    )(*ins)


def group_slots():
    y, c, s = lax.axis_index("y"), lax.axis_index("c"), lax.axis_index("s")
    r = jnp.arange(16, dtype=jnp.int32)
    core = c ^ (r // 8)
    row = (y + (r // 2) % 4) % 4
    part = s ^ (r % 2)
    return (row * 2 + core) * 2 + part


def load_rows(places, which, near, far, width, target, sems):
    copies = []
    for r in range(16):
        origin = (near if r < 8 else far).at[r % 8, :, pl.ds(0, width)]
        start = pl.multiple_of(places[which, r] * 128, 128)
        copies.append(pltpu.make_async_copy(origin, target.at[pl.ds(start, 128)], sems.at[r]))
    return copies


def load_hidden(order, which, blocks, target, sems):
    copies = []
    for j in range(16):
        start = pl.multiple_of(order[which, j] * 128, 128)
        origin = blocks.at[j, pl.ds(which * 128, 128)]
        copies.append(pltpu.make_async_copy(origin, target.at[pl.ds(start, 128)], sems.at[j]))
    return copies


def load_out(places, near, far, target, sems):
    copies = []
    for r in range(16):
        for half in range(2):
            origin = (near if r < 8 else far).at[r % 8, :, pl.ds(768 + half * 128, 128)]
            start = pl.multiple_of(places[1, r] * 128, 128)
            copies.append(
                pltpu.make_async_copy(
                    origin,
                    target.at[pl.ds(half * 128, 128), pl.ds(start, 128)],
                    sems.at[r * 2 + half],
                )
            )
    return copies


def at_first(copies):
    @pl.when(pl.program_id(0) == 0)
    def _():
        for copy in copies:
            copy.start()
        for copy in copies:
            copy.wait()


def norm_kernel(x_ref, vec_ref, one_ref, two_ref, one_flip, two_flip, mean_ref, inverse_ref):
    field = wide(x_ref[...])
    mean = jnp.mean(field, axis=-1, keepdims=True)
    center = field - mean
    inverse = lax.rsqrt(jnp.mean(center * center, axis=-1, keepdims=True) + ln_eps)
    unit = center * inverse
    one = low(unit * vec_ref[0:1, :] + vec_ref[1:2, :])
    two = low(unit * vec_ref[2:3, :] + vec_ref[3:4, :])
    one_ref[...] = one
    two_ref[...] = two
    one_flip[...] = one.T
    two_flip[...] = two.T
    mean_ref[...] = mean
    inverse_ref[...] = inverse


def place_kernel(places, order, near, far, blocks, out_ref, up_ref, down_ref, w_out, w_up, w_down, sems, more):
    sets = (
        (load_out(places, near, far, w_out, sems), w_out, out_ref),
        (load_hidden(order, 0, blocks, w_up, more.at[0]), w_up, up_ref),
        (load_hidden(order, 1, blocks, w_down, more.at[1]), w_down, down_ref),
    )
    for copies, _, _ in sets:
        for copy in copies:
            copy.start()
    outward = []
    for k, (copies, held, target) in enumerate(sets):
        for copy in copies:
            copy.wait()
        outward.append(pltpu.make_async_copy(held, target, more.at[2, k]))
        outward[-1].start()
    for copy in outward:
        copy.wait()


def turn(field, table, way):
    head = field[:, :128]
    lane = lax.broadcasted_iota(jnp.int32, (1, 128), 1)
    cosine = jnp.where(lane < 64, table, 1.0)
    sine = jnp.where(lane < 64, pltpu.roll(table, 64, 1), 0.0)
    moved = jnp.where(lane < 32, pltpu.roll(head, 96, 1), pltpu.roll(head, 32, 1)) * sine
    return jnp.concatenate([head * cosine + way * moved, field[:, 128:]], axis=1)


def qkv_kernel(
    places, h_ref, near, far, bias_ref, table_ref, q_ref, k_ref, v_ref, w_ref, weight, sems, last
):
    at_first(load_rows(places, 0, near, far, 768, weight, sems))
    keep = pltpu.make_async_copy(weight, w_ref, last)

    @pl.when(pl.program_id(0) == 0)
    def _():
        keep.start()

    raw = mxu(h_ref[...], weight[...], NN) + bias_ref[...]
    table = table_ref[...]
    q_ref[...] = low(turn(raw[:, :256], table, 1.0))
    k_ref[...] = low(turn(raw[:, 256:512], table, 1.0))
    v_ref[...] = low(raw[:, 512:])

    @pl.when(pl.program_id(0) == pl.num_programs(0) - 1)
    def _():
        keep.wait()


def up_kernel(h_ref, w_ref, bias_ref, hidden_ref, slope_ref, flip_ref):
    pre = mxu(h_ref[...], w_ref[...], NN) + bias_ref[...]
    share = 0.5 * (1.0 + lax.erf(pre * 0.7071067811865476))
    hidden = low(pre * share)
    hidden_ref[...] = hidden
    flip_ref[...] = hidden.T
    slope_ref[...] = share + pre * (jnp.exp(-0.5 * pre * pre) * 0.3989422804014327)


def attention_kernel(
    lens,
    q_ref,
    k_ref,
    v_ref,
    fk_ref,
    fv_ref,
    dy_ref,
    w_ref,
    table_ref,
    att_ref,
    flip_ref,
    dq_ref,
    dkv_ref,
    dfk_ref,
    dfv_ref,
    flipped,
    total,
):
    step = pl.program_id(0)
    scale = 0.0625

    @pl.when(step == 0)
    def _():
        for part, refs in enumerate(((k_ref, v_ref), (fk_ref, fv_ref))):
            for which in range(2):
                flipped[which, :, pl.ds(part * ROWS, ROWS)] = refs[which][...].T
        total[...] = jnp.zeros_like(total)

    first, second, part = lens[0], lens[1], lens[2]

    def tile(extent):
        query = low(wide(q_ref[...]) * scale)
        q_index = lax.broadcasted_iota(jnp.int32, (1, TILE), 1) + (extent - TILE)
        q_seg = jnp.where(q_index < first, 0, 1)
        q_pos = jnp.where(q_index < first, first + q_index, second + q_index - first)

        k_index = lax.broadcasted_iota(jnp.int32, (extent, 1), 0)
        own_seen = (jnp.where(k_index < first, 0, 1) == q_seg) & (k_index <= q_index)
        f_index = lax.broadcasted_iota(jnp.int32, (ROWS, 1), 0)
        f_seg = jnp.where(part == 1, jnp.where(f_index < first, 0, 1), 2)
        f_pos = jnp.where(f_index < first, f_index, f_index - first)
        far_seen = (f_seg == q_seg) & (f_pos <= q_pos)

        own = jnp.where(own_seen, mxu(k_ref[:extent], query, NT), -1e30)
        other = jnp.where(far_seen, mxu(fk_ref[...], query, NT), -1e30)
        grad = low(mxu(dy_ref[...], w_ref[...], NT))
        top = jnp.maximum(
            jnp.max(own, axis=0, keepdims=True), jnp.max(other, axis=0, keepdims=True)
        )
        own = jnp.exp(own - top)
        other = jnp.exp(other - top)
        bottom = 1.0 / (
            jnp.sum(own, axis=0, keepdims=True) + jnp.sum(other, axis=0, keepdims=True)
        )
        own = own * bottom
        other = other * bottom
        own_low, other_low = low(own), low(other)
        own_grad = mxu(v_ref[:extent], grad, NT)
        other_grad = mxu(fv_ref[...], grad, NT)
        attended = mxu(flipped[1, :, :extent], own_low, NN) + mxu(
            flipped[1, :, ROWS:], other_low, NN
        )
        flip_ref[...] = low(attended)
        att_ref[...] = low(attended.T)
        total[1, :extent] += mxu(own_low, grad, NN)
        total[1, ROWS:] += mxu(other_low, grad, NN)
        inner = jnp.sum(own * own_grad, axis=0, keepdims=True) + jnp.sum(
            other * other_grad, axis=0, keepdims=True
        )
        own_low = low(own * (own_grad - inner))
        other_low = low(other * (other_grad - inner))
        total[0, :extent] += mxu(own_low, query, NN)
        total[0, ROWS:] += mxu(other_low, query, NN)
        turned_grad = mxu(flipped[0, :, :extent], own_low, NN) + mxu(
            flipped[0, :, ROWS:], other_low, NN
        )
        dq_ref[...] = low(turn(turned_grad.T * scale, table_ref[...], -1.0))

    for number in range(ROWS // TILE):

        @pl.when(step == number)
        def _():
            tile((number + 1) * TILE)

    @pl.when(step == pl.num_programs(0) - 1)
    def _():
        dkv_ref[...] = total[:, :ROWS]
        dfk_ref[...] = low(total[0, ROWS:])
        dfv_ref[...] = low(total[1, ROWS:])


def finish_kernel(dq_ref, dkv_ref, fk_ref, fv_ref, table_ref, out_ref):
    out_ref[:, :256] = dq_ref[...]
    out_ref[:, 256:512] = low(turn(dkv_ref[0] + wide(fk_ref[...]), table_ref[...], -1.0))
    out_ref[:, 512:] = low(dkv_ref[1] + wide(fv_ref[...]))


def branch_kernel(att_ref, hidden_ref, out_w, down_w, out_ref):
    out_ref[...] = low(mxu(att_ref[...], out_w[...], NN) + mxu(hidden_ref[...], down_w[...], NT))


def slope_kernel(dy_ref, down_w, slope_ref, out_ref):
    out_ref[...] = low(mxu(dy_ref[...], down_w[...], NN) * slope_ref[...])


def unit_kernel(
    first, x_ref, mean_ref, inverse_ref, dqkv_ref, dpre_ref, vec_ref, bias_ref, w_qkv, w_up,
    out_1, out_2, out_3, out_0, sum_ref, result, split_ref,
):
    step = pl.program_id(0)

    @pl.when(step == 0)
    def _():
        split_ref[:, :768] = jnp.sum(wide(dqkv_ref[...]), axis=0, keepdims=True)
        split_ref[:, 768:1792] = jnp.sum(wide(dpre_ref[...]), axis=0, keepdims=True)
        split_ref[:, 1792:] = jnp.zeros((1, 256), f32)

    unit = (wide(x_ref[...]) - mean_ref[...]) * inverse_ref[...]
    one = mxu(dqkv_ref[...], w_qkv[...], NT)
    two = mxu(dpre_ref[...], w_up[...], NT)
    result[...] = low(one * vec_ref[0:1, :] + two * vec_ref[2:3, :])
    sum_ref[0:1, :] = jnp.sum(one * unit, axis=0, keepdims=True)
    sum_ref[1:2, :] = jnp.sum(one, axis=0, keepdims=True)
    sum_ref[2:3, :] = jnp.sum(two * unit, axis=0, keepdims=True)
    sum_ref[3:4, :] = jnp.sum(two, axis=0, keepdims=True)
    sum_ref[4:5, :] = bias_ref[...]
    sum_ref[5:6, :] = split_ref[:, pl.ds(pl.multiple_of(step * 512, 512), 512)]
    sum_ref[6:8, :] = jnp.zeros((2, 512), f32)
    for number, ref in enumerate((out_1, out_2, out_3, out_0)):
        start = pl.multiple_of((first[0] + number) % 4 * 256, 256)
        ref[...] = result[pl.ds(start, 256), :]


def column_grads_kernel(places, att_ref, hidden_ref, d0, d1, d2, d3, o0, o1, o2, o3, far_ref, near_ref):
    step = pl.program_id(0)
    down = low(
        mxu(hidden_ref[...], jnp.concatenate([d0[...], d1[...], d2[...], d3[...]], axis=1), NN)
    )
    out = low(mxu(att_ref[...], jnp.concatenate([o0[...], o1[...], o2[...], o3[...]], axis=1), NN))
    for when, ref in ((step < 2, far_ref), (step >= 2, near_ref)):

        @pl.when(when)
        def _():
            for k in range(4):
                ref[k, :1024] = down[:, k * 128 : k * 128 + 128]
                ref[k, 1024:] = out[:, k * 128 : k * 128 + 128]


def row_grads_kernel(places, a0, a1, a2, a3, b0, b1, b2, b3, dqkv_ref, dpre_ref, far_ref, near_ref):
    step = pl.program_id(0)
    qkv = low(mxu(jnp.concatenate([a0[...], a1[...], a2[...], a3[...]], axis=0), dqkv_ref[...], NN))
    up = low(mxu(jnp.concatenate([b0[...], b1[...], b2[...], b3[...]], axis=0), dpre_ref[...], NN))
    for when, ref in ((step < 2, far_ref), (step >= 2, near_ref)):

        @pl.when(when)
        def _():
            for k in range(4):
                ref[k, :, :768] = qkv[k * 128 : k * 128 + 128]
                ref[k, :, 768:] = up[k * 128 : k * 128 + 128]


def fixed(*shape):
    return pl.BlockSpec(shape, lambda i, *_: (0,) * len(shape))


def led(kernel, steps, lead, ins, in_specs, outs, out_specs, scratch, flops, moved):
    return pl.pallas_call(
        kernel,
        name=kernel.__name__,
        grid_spec=pltpu.PrefetchScalarGridSpec(
            num_scalar_prefetch=1,
            grid=(steps,),
            in_specs=in_specs,
            out_specs=out_specs,
            scratch_shapes=scratch,
        ),
        out_shape=outs,
        compiler_params=pltpu.CompilerParams(vmem_limit_bytes=60 * 2**20),
        cost_estimate=pl.CostEstimate(flops=flops, bytes_accessed=moved, transcendentals=0),
    )(lead, *ins)


def run_norm(tokens, shared_vec):
    return run(
        norm_kernel,
        4,
        (tokens, shared_vec),
        [tiled(256, 2048), whole(6, 2048)],
        [struct((ROWS, 2048), bf16)] * 2
        + [struct((2048, ROWS), bf16)] * 2
        + [struct((ROWS, 1), f32)] * 2,
        [tiled(256, 2048)] * 2
        + [pl.BlockSpec((2048, 256), lambda i: (0, i))] * 2
        + [tiled(256, 1)] * 2,
        [],
        2**24,
        20 * 2**20,
    )


def run_qkv(places, h_one, near, far, bias, table):
    return run(
        qkv_kernel,
        ROWS // TILE,
        (places, h_one, near, far, bias, table),
        [SCALARS, tiled(TILE, 2048), ANY, ANY, whole(1, 768), tiled(TILE, 128)],
        [struct((ROWS, 256), bf16)] * 3 + [struct((2048, 768), bf16)],
        [tiled(TILE, 256)] * 3 + [ANY],
        [pltpu.VMEM((2048, 768), bf16), pltpu.SemaphoreType.DMA((16,)), pltpu.SemaphoreType.DMA],
        2 * ROWS * 2048 * 768,
        9 * 2**20,
    )


def run_place(places, order, near, far, blocks):
    dma = pltpu.SemaphoreType.DMA
    shapes = ((256, 2048), (2048, 1024), (2048, 1024))
    return run(
        place_kernel,
        1,
        (places, order, near, far, blocks),
        [SCALARS, SCALARS, ANY, ANY, ANY],
        [struct(shape, bf16) for shape in shapes],
        [ANY] * 3,
        [pltpu.VMEM(shape, bf16) for shape in shapes] + [dma((32,)), dma((3, 16))],
        1,
        18 * 2**20,
    )


def run_up(h_two, w_up, bias):
    return run(
        up_kernel,
        ROWS // TILE,
        (h_two, w_up, bias),
        [tiled(TILE, 2048), whole(2048, 1024), whole(1, 1024)],
        [struct((ROWS, 1024), bf16), struct((ROWS, 1024), f32), struct((1024, ROWS), bf16)],
        [tiled(TILE, 1024)] * 2 + [pl.BlockSpec((1024, TILE), lambda i: (0, i))],
        [],
        2 * ROWS * 2048 * 1024,
        16 * 2**20,
    )


def run_attention(lens, query, key, value, far_key, far_value, cotangent, w_out, table):
    return run(
        attention_kernel,
        ROWS // TILE,
        (lens, query, key, value, far_key, far_value, cotangent, w_out, table),
        [SCALARS, tiled(TILE, 256)]
        + [whole(ROWS, 256)] * 4
        + [tiled(TILE, 2048), whole(256, 2048), tiled(TILE, 128)],
        [struct((ROWS, 256), bf16), struct((256, ROWS), bf16), struct((ROWS, 256), bf16)]
        + [struct((2, ROWS, 256), f32)]
        + [struct((ROWS, 256), bf16)] * 2,
        [tiled(TILE, 256), pl.BlockSpec((256, TILE), lambda i: (0, i)), tiled(TILE, 256)]
        + [whole(2, ROWS, 256)]
        + [whole(ROWS, 256)] * 2,
        [pltpu.VMEM((2, 256, 2 * ROWS), bf16), pltpu.VMEM((2, 2 * ROWS, 256), f32)],
        8 * 2**30,
        12 * 2**20,
    )


def run_branch(attended, hidden, w_out, w_down):
    return run(
        branch_kernel,
        ROWS // TILE,
        (attended, hidden, w_out, w_down),
        [tiled(TILE, 256), tiled(TILE, 1024), whole(256, 2048), whole(2048, 1024)],
        struct((ROWS, 2048), bf16),
        tiled(TILE, 2048),
        [],
        2 * ROWS * 2048 * 1280,
        12 * 2**20,
    )


def run_slope(cotangent, w_down, slope):
    return run(
        slope_kernel,
        ROWS // TILE,
        (cotangent, w_down, slope),
        [tiled(TILE, 2048), whole(2048, 1024), tiled(TILE, 1024)],
        struct((ROWS, 1024), bf16),
        tiled(TILE, 1024),
        [],
        2 * ROWS * 2048 * 1024,
        14 * 2**20,
    )


def run_finish(grad_query, grad_kv, far_gkey, far_gvalue, table):
    kv_spec = pl.BlockSpec((2, 512, 256), lambda i: (0, i, 0))
    return run(
        finish_kernel,
        2,
        (grad_query, grad_kv, far_gkey, far_gvalue, table),
        [tiled(512, 256), kv_spec] + [tiled(512, 256)] * 2 + [tiled(512, 128)],
        struct((ROWS, 768), bf16),
        tiled(512, 768),
        [],
        2**20,
        6 * 2**20,
    )


def run_unit(first, tokens, mean, inverse, grad_qkv, grad_pre, shared_vec, bias_sum, w_qkv, w_up):
    def chunk(rows):
        return pl.BlockSpec((rows, 512), lambda i, lead: (0, i))

    return led(
        unit_kernel,
        4,
        first,
        (tokens, mean, inverse, grad_qkv, grad_pre, shared_vec, bias_sum, w_qkv, w_up),
        [chunk(ROWS), fixed(ROWS, 1), fixed(ROWS, 1), fixed(ROWS, 768), fixed(ROWS, 1024), chunk(6), chunk(1)]
        + [pl.BlockSpec((512, width), lambda i, lead: (i, 0)) for width in (768, 1024)],
        [struct((256, 2048), bf16)] * 4 + [struct((8, 2048), f32)],
        [chunk(256)] * 4 + [chunk(8)],
        [pltpu.VMEM((ROWS, 512), bf16), pltpu.VMEM((1, 2048), f32)],
        2 * ROWS * 2048 * 1792,
        20 * 2**20,
    )


def run_column_grads(places, att_flip, hidden_flip, cotangent):
    def block(which, k):
        return pl.BlockSpec((ROWS, 128), lambda i, p: (0, p[which, (i * 4 + 8 + k) % 16]))

    return led(
        column_grads_kernel,
        4,
        places,
        (att_flip, hidden_flip) + (cotangent,) * 8,
        [fixed(256, ROWS), fixed(1024, ROWS)]
        + [block(3, k) for k in range(4)]
        + [block(1, k) for k in range(4)],
        [struct((8, 1280, 128), bf16)] * 2,
        [
            pl.BlockSpec((4, 1280, 128), lambda i, p: (jnp.minimum(i, 1), 0, 0)),
            pl.BlockSpec((4, 1280, 128), lambda i, p: (jnp.maximum(i - 2, 0), 0, 0)),
        ],
        [],
        2 * ROWS * 2048 * 1280,
        12 * 2**20,
    )


def run_row_grads(places, one_flip, two_flip, grad_qkv, grad_pre):
    def block(which, k):
        return pl.BlockSpec((128, ROWS), lambda i, p: (p[which, (i * 4 + 8 + k) % 16], 0))

    return led(
        row_grads_kernel,
        4,
        places,
        (one_flip,) * 4 + (two_flip,) * 4 + (grad_qkv, grad_pre),
        [block(0, k) for k in range(4)]
        + [block(2, k) for k in range(4)]
        + [fixed(ROWS, 768), fixed(ROWS, 1024)],
        [struct((8, 128, 1792), bf16)] * 2,
        [
            pl.BlockSpec((4, 128, 1792), lambda i, p: (jnp.minimum(i, 1), 0, 0)),
            pl.BlockSpec((4, 128, 1792), lambda i, p: (jnp.maximum(i - 2, 0), 0, 0)),
        ],
        [],
        2 * ROWS * 2048 * 1792,
        16 * 2**20,
    )


def lay_kernel(starts, *refs):
    ins, out, hold, in_sems, out_sems = refs[:-4], refs[-4], refs[-3], refs[-2], refs[-1]
    inward, outward = [], []
    low = 0
    for k, ref in enumerate(ins):
        size = ref.shape[0]
        spot = hold.at[pl.ds(low, size)]
        low += size
        target = out.at[pl.ds(pl.multiple_of(starts[k] * 128, 128), size)]
        inward.append(pltpu.make_async_copy(ref, spot, in_sems.at[k]))
        outward.append(pltpu.make_async_copy(spot, target, out_sems.at[k]))
    for copy in inward:
        copy.start()
    for first, second in zip(inward, outward):
        first.wait()
        second.start()
    for copy in outward:
        copy.wait()


def copy_kernel(source, out, hold_ref, in_sems, out_sems):
    inward, outward = [], []
    for k in range(8):
        spot = pl.ds(k * 128, 128)
        inward.append(pltpu.make_async_copy(source.at[spot], hold_ref.at[spot], in_sems.at[k]))
        outward.append(pltpu.make_async_copy(hold_ref.at[spot], out.at[spot], out_sems.at[k]))
    for copy in inward:
        copy.start()
    for first, second in zip(inward, outward):
        first.wait()
        second.start()
    for copy in outward:
        copy.wait()


def copy_rows(field):
    return pl.pallas_call(
        copy_kernel,
        name="copy_kernel",
        out_shape=struct(field.shape, field.dtype),
        in_specs=[ANY],
        out_specs=ANY,
        scratch_shapes=[
            pltpu.VMEM(field.shape, field.dtype),
            pltpu.SemaphoreType.DMA((8,)),
            pltpu.SemaphoreType.DMA((8,)),
        ],
        compiler_params=pltpu.CompilerParams(vmem_limit_bytes=32 * 2**20),
    )(field)


def lay_rows(x, pieces):
    far = ((x + 2) % 4) * 2
    starts = jnp.stack([x * 2, ((x + 1) % 4) * 2, far, far + 1, ((x + 3) % 4) * 2])
    width, dtype = pieces[0].shape[1], pieces[0].dtype
    return pl.pallas_call(
        lay_kernel,
        name="lay_kernel",
        out_shape=struct((ROWS, width), dtype),
        in_specs=[SCALARS] + [ANY] * 5,
        out_specs=ANY,
        scratch_shapes=[
            pltpu.VMEM((ROWS, width), dtype),
            pltpu.SemaphoreType.DMA((5,)),
            pltpu.SemaphoreType.DMA((5,)),
        ],
        compiler_params=pltpu.CompilerParams(vmem_limit_bytes=32 * 2**20),
    )(starts, *pieces)


def up_y(values):
    return lax.ppermute(values, "y", UP)


def down_y(values):
    return lax.ppermute(values, "y", DOWN)


def up_x(values):
    return lax.ppermute(values, "x", UP)


def down_x(values):
    return lax.ppermute(values, "x", DOWN)


def swap(values, axis):
    return lax.ppermute(values, axis, PAIR)


def hold(values):
    return lax.optimization_barrier(values)


def join(*parts):
    return jnp.concatenate(parts, axis=0)


def per_device(
    tokens,
    cotangent,
    seq_lens,
    owners,
    shared_vec,
    shared_first,
    shared_second,
    split_vec,
    split_first,
    split_second,
    qkv_master,
    qkv_first,
    qkv_second,
    qkv_left,
    qkv_right,
    out_master,
    out_first,
    out_second,
    out_left,
    out_right,
    up_master,
    up_first,
    up_second,
    up_left,
    up_right,
    down_master,
    down_first,
    down_second,
    down_left,
    down_right,
):
    part = lax.axis_index("s")
    x, z = lax.axis_index("x"), lax.axis_index("z")

    out_block = out_master.reshape(256, 128)
    packed = low(jnp.concatenate([qkv_master[0], out_block[:128], out_block[128:]], axis=1))[None]
    partner = swap(packed, "s")
    hidden_own = low(join(up_master[0], down_master.reshape(1024, 128).T))[None]
    blocks = lax.all_gather(hidden_own, GROUP_AXES, axis=0, tiled=True)
    h_one, h_two, one_flip, two_flip, mean, inverse = run_norm(tokens, shared_vec)
    lens = jnp.stack([seq_lens[0, 0] // 2, seq_lens[0, 1] // 2, part.astype(jnp.int32)])
    local_index = jnp.arange(ROWS, dtype=jnp.int32)
    _, position = row_places(seq_lens[0, 0], seq_lens[0, 1], part, local_index, 2)
    partner, h_one, h_two, one_flip, two_flip, mean, inverse, lens, position = hold(
        (partner, h_one, h_two, one_flip, two_flip, mean, inverse, lens, position)
    )
    bias_sum = jnp.sum(wide(cotangent), axis=0, keepdims=True) * 0.125
    pair = join(packed, partner)
    before, after = up_y(pair), down_y(pair)
    slots = group_slots()
    ids = jnp.arange(16, dtype=jnp.int32)
    places = jnp.sum(
        jnp.where(owners[:, None, :] == slots[None, :, None], ids[None, None, :], 0), axis=2
    )
    order = jnp.sum(jnp.where(owners[2:, None, :] == ids[None, :, None], ids, 0), axis=2)
    frequency = 10000.0 ** (-2.0 * jnp.arange(32, dtype=f32) / 64)
    angles = position.astype(f32)[:, None] * frequency[None, :]
    cosine, sine_part = jnp.cos(angles), jnp.sin(angles)
    table = jnp.concatenate([cosine, cosine, -sine_part, sine_part], axis=1)
    bias_qkv, bias_up = split_vec[:, :768], split_vec[:, 768:]

    (
        before, after, h_one, h_two, places, order, lens, table, bias_qkv, bias_up, bias_sum,
    ) = hold((
        before, after, h_one, h_two, places, order, lens, table, bias_qkv, bias_up, bias_sum,
    ))
    far_a, far_b = up_y(before[0:1]), down_y(after[1:2])
    far_a, far_b = hold((far_a, far_b))
    near = join(pair, after, far_a, far_b, before)
    far = swap(near, "c")
    query, key, value, w_qkv = run_qkv(places, h_one, near, far, bias_qkv, table)
    far_key = lax.ppermute(key, "s", [(0, 1)])
    far_value = lax.ppermute(value, "s", [(0, 1)])
    w_out, w_up, w_down = run_place(places, order, near, far, blocks)
    hidden, slope, hidden_flip = run_up(h_two, w_up, bias_up)
    far_key, far_value, hidden, slope, hidden_flip = hold(
        (far_key, far_value, hidden, slope, hidden_flip)
    )
    attended, att_flip, grad_query, grad_kv, far_gkey, far_gvalue = run_attention(
        lens, query, key, value, far_key, far_value, cotangent, w_out, table
    )
    attended, far_gkey, far_gvalue = hold((attended, far_gkey, far_gvalue))
    far_gkey = lax.ppermute(far_gkey, "s", [(1, 0)])
    partial_out = run_branch(attended, hidden, w_out, w_down)
    partial_out, slope = hold((partial_out, slope))
    part_sum = lax.psum_scatter(partial_out, "x", scatter_dimension=0, tiled=True)
    grad_pre = run_slope(cotangent, w_down, slope)
    grad_pre, far_gkey, far_gvalue, hidden_flip = hold((grad_pre, far_gkey, far_gvalue, hidden_flip))
    far_gvalue = lax.ppermute(far_gvalue, "s", [(1, 0)])
    column_far, column_near = run_column_grads(places, att_flip, hidden_flip, cotangent)
    column_far, column_near, grad_query, far_gvalue = hold(
        (column_far, column_near, grad_query, far_gvalue)
    )
    column_twin = swap(column_far, "c")
    grad_qkv = run_finish(grad_query, grad_kv, far_gkey, far_gvalue, table)
    column_twin, grad_qkv = hold((column_twin, grad_qkv))

    def both(pair, start, stop):
        return wide(pair[0][start:stop]) + wide(pair[1][start:stop])

    def first_hop(pair):
        return up_y(low(both(pair, 4, 5))), down_y(low(both(pair, 5, 6)))

    def second_hop(pair, first, last):
        ahead = up_y(low(join(both(pair, 2, 3) + wide(first), both(pair, 3, 4))))
        behind = down_y(low(join(both(pair, 6, 7), both(pair, 7, 8) + wide(last))))
        return ahead, behind

    def last_hop(pair, ahead, behind):
        total = both(pair, 0, 2) + wide(ahead) + wide(behind)
        return total[0] + wide(swap(low(total[1]), "s"))

    columns = (column_near, column_twin)
    column_a, column_b = first_hop(columns)
    unit_1, unit_2, unit_3, unit_0, sums = run_unit(
        jnp.stack([x + 1]).astype(jnp.int32),
        tokens,
        mean,
        inverse,
        grad_qkv,
        grad_pre,
        shared_vec,
        bias_sum,
        w_qkv,
        w_up,
    )

    def own(values_in):
        return wide(lax.dynamic_slice_in_dim(values_in, (x * 2 + z) * 128, 128, axis=0))

    def half(values, which):
        return lax.dynamic_slice_in_dim(values, which * 128, 128, axis=0)

    def both_rows(mine, theirs):
        return join(jnp.where(z == 0, mine, theirs), jnp.where(z == 0, theirs, mine))

    near_y = [(i, i ^ 1) for i in range(4)]
    far_y = [(i, i ^ 2) for i in range(4)]

    unit_1, unit_2, unit_3, unit_0, sums, column_a, column_b, grad_pre, part_sum = hold(
        (unit_1, unit_2, unit_3, unit_0, sums, column_a, column_b, grad_pre, part_sum)
    )
    unit_1, unit_3 = up_x(unit_1), down_x(unit_3)
    unit_2a = lax.ppermute(unit_2[:128], "x", far_y)
    out_partner = swap(half(part_sum, 1 - z), "z")
    column_prev, column_next = second_hop(columns, column_a, column_b)
    row_far, row_near = run_row_grads(places, one_flip, two_flip, grad_qkv, grad_pre)
    unit_1, unit_2a, unit_3, out_partner, row_far, row_near, column_prev, column_next = hold(
        (unit_1, unit_2a, unit_3, out_partner, row_far, row_near, column_prev, column_next)
    )
    unit_2b = lax.ppermute(unit_2[128:], "x", far_y)
    rows = (row_near, swap(row_far, "c"))
    row_a, row_b = first_hop(rows)
    out_rows = low(
        own(tokens) + wide(half(part_sum, z)) + wide(out_partner) + shared_vec[4] + shared_vec[5]
    )
    out_twin = swap(out_rows, "z")
    column_sum = last_hop(columns, column_prev, column_next)
    sums = sums + swap(sums, "c")
    total = wide(unit_0) + wide(unit_1) + wide(unit_3)
    unit_2b, total, rows, row_a, row_b, out_rows, out_twin, column_sum, sums = hold(
        (unit_2b, total, rows, row_a, row_b, out_rows, out_twin, column_sum, sums)
    )
    output = lax.all_gather(both_rows(out_rows, out_twin), "x", axis=0, tiled=True)
    total = total + wide(join(unit_2a, unit_2b))
    own_grad = half(total, z) + wide(swap(low(half(total, 1 - z)), "z"))
    row_prev, row_next = second_hop(rows, row_a, row_b)
    sums = sums + swap(sums, "s")
    new_down = soap_block(
        column_sum[:1024],
        down_master[:, 0],
        down_first[:, 0],
        down_second[:, 0],
        down_left[0, 0],
        down_right[0, 0],
        rate_down,
    )
    own_grad, row_prev, row_next, sums, new_down = hold((own_grad, row_prev, row_next, sums, new_down))
    own_inverse = lax.dynamic_slice_in_dim(inverse, (x * 2 + z) * 128, 128, axis=0)
    own_mean = lax.dynamic_slice_in_dim(mean, (x * 2 + z) * 128, 128, axis=0)
    own_unit = (own(tokens) - own_mean) * own_inverse
    grad_x = (
        own_grad
        - jnp.mean(own_grad, axis=-1, keepdims=True)
        - own_unit * jnp.mean(own_grad * own_unit, axis=-1, keepdims=True)
    ) * own_inverse
    grad_rows = low(own(cotangent) + grad_x)
    grad_twin = swap(grad_rows, "z")
    row_sum = last_hop(rows, row_prev, row_next)
    sums = sums + lax.ppermute(sums, "y", near_y)
    new_out = soap_block(
        column_sum[1024:],
        out_master[:, 0],
        out_first[:, 0],
        out_second[:, 0],
        out_left[0, 0],
        out_right[0, 0],
        rate_out,
    )
    grad_rows, grad_twin, row_sum, sums, new_out = hold((grad_rows, grad_twin, row_sum, sums, new_out))
    grad_pair = both_rows(grad_rows, grad_twin)
    grad_before, grad_after = up_x(grad_pair), down_x(grad_pair)
    sums = sums + lax.ppermute(sums, "y", far_y)
    shared_sum = sums + swap(sums, "z")
    shared_sum = shared_sum + lax.ppermute(shared_sum, "x", near_y)
    new_qkv = soap_block(
        row_sum[:, :768],
        qkv_master[0],
        qkv_first[0],
        qkv_second[0],
        qkv_left[0, 0],
        qkv_right[0, 0],
        rate_qkv,
    )
    new_up = soap_block(
        row_sum[:, 768:], up_master[0], up_first[0], up_second[0], up_left[0, 0], up_right[0, 0], rate_up
    )
    grad_before, grad_after, grad_pair, shared_sum, new_qkv, new_up, output = hold(
        (grad_before, grad_after, grad_pair, shared_sum, new_qkv, new_up, output)
    )
    far_a, far_b = up_x(grad_before[:128]), down_x(grad_after[128:])
    shared_sum = shared_sum + lax.ppermute(shared_sum, "x", far_y)
    output = copy_rows(output)
    far_a, far_b, shared_sum, output = hold((far_a, far_b, shared_sum, output))
    grad_input = lay_rows(x, [grad_pair, grad_after, far_a, far_b, grad_before])
    split_grad = sums[5:6, :1792]
    shared_grad = join(shared_sum[:5], shared_sum[4:5])
    new_shared = adam_vector(shared_grad, shared_vec, shared_first, shared_second)
    new_split = adam_vector(split_grad, split_vec, split_first, split_second)
    return (
        output,
        grad_input,
        new_shared[0],
        new_shared[1],
        new_shared[2],
        new_split[0],
        new_split[1],
        new_split[2],
        new_qkv[0][None],
        new_qkv[1][None],
        new_qkv[2][None],
        new_qkv[0][None].astype(bf16),
        new_out[0][:, None],
        new_out[1][:, None],
        new_out[2][:, None],
        new_out[0][:, None].astype(bf16),
        new_up[0][None],
        new_up[1][None],
        new_up[2][None],
        new_up[0][None].astype(bf16),
        new_down[0][:, None],
        new_down[1][:, None],
        new_down[2][:, None],
        new_down[0][:, None].astype(bf16),
    )


def solution(mesh):
    in_specs = (
        P(("y", "c", "s"), None),
        P(("y", "c", "s"), None),
        P(("y", "c"), None),
        P(),
        P(),
        P(),
        P(),
        P(("x", "z"), None),
        P(("x", "z"), None),
        P(("x", "z"), None),
        P(("y", "c", "s"), None, ("x", "z")),
        P(("y", "c", "s"), None, ("x", "z")),
        P(("y", "c", "s"), None, ("x", "z")),
        P(("y", "c", "s"), ("x", "z"), None, None),
        P(("y", "c", "s"), ("x", "z"), None, None),
        P(("x", "z"), ("y", "c", "s"), None),
        P(("x", "z"), ("y", "c", "s"), None),
        P(("x", "z"), ("y", "c", "s"), None),
        P(("y", "c", "s"), ("x", "z"), None, None),
        P(("y", "c", "s"), ("x", "z"), None, None),
        P(("y", "c", "s"), None, ("x", "z")),
        P(("y", "c", "s"), None, ("x", "z")),
        P(("y", "c", "s"), None, ("x", "z")),
        P(("y", "c", "s"), ("x", "z"), None, None),
        P(("y", "c", "s"), ("x", "z"), None, None),
        P(("x", "z"), ("y", "c", "s"), None),
        P(("x", "z"), ("y", "c", "s"), None),
        P(("x", "z"), ("y", "c", "s"), None),
        P(("y", "c", "s"), ("x", "z"), None, None),
        P(("y", "c", "s"), ("x", "z"), None, None),
    )
    out_specs = (
        P(("y", "c", "s"), None),
        P(("y", "c", "s"), None),
        P(),
        P(),
        P(),
        P(("x", "z"), None),
        P(("x", "z"), None),
        P(("x", "z"), None),
        P(("y", "c", "s"), None, ("x", "z")),
        P(("y", "c", "s"), None, ("x", "z")),
        P(("y", "c", "s"), None, ("x", "z")),
        P(("y", "c", "s"), None, ("x", "z")),
        P(("x", "z"), ("y", "c", "s"), None),
        P(("x", "z"), ("y", "c", "s"), None),
        P(("x", "z"), ("y", "c", "s"), None),
        P(("x", "z"), ("y", "c", "s"), None),
        P(("y", "c", "s"), None, ("x", "z")),
        P(("y", "c", "s"), None, ("x", "z")),
        P(("y", "c", "s"), None, ("x", "z")),
        P(("y", "c", "s"), None, ("x", "z")),
        P(("x", "z"), ("y", "c", "s"), None),
        P(("x", "z"), ("y", "c", "s"), None),
        P(("x", "z"), ("y", "c", "s"), None),
        P(("x", "z"), ("y", "c", "s"), None),
    )
    fine = Mesh(mesh.devices.reshape(4, 2, 2, 4, 2), ("y", "c", "s", "x", "z"))
    return jax.shard_map(
        per_device, mesh=fine, in_specs=in_specs, out_specs=out_specs, check_vma=False
    )
```

```python
import jax
import jax.numpy as jnp
from jax import lax
from jax.experimental import pallas as pl
from jax.experimental.pallas import tpu as pltpu
from jax.sharding import Mesh, PartitionSpec as P

D = 2048
H = 8
STEP = 5


ln_eps = 1e-05
adam_eps = 1e-08
beta_one = 0.5
beta_two = 0.5
rate_qkv = 0.01
rate_out = 0.05
rate_up = 0.01
rate_down = 0.005
rate_vector = 0.2
weight_decay = 0.01


def exact_dot(left_matrix, right_matrix):
    return jnp.dot(
        left_matrix,
        right_matrix,
        precision=lax.Precision.HIGH,
        preferred_element_type=jnp.float32,
    )


def contract_rows(left_matrix, right_matrix):
    return lax.dot_general(
        left_matrix, right_matrix, (((0,), (0,)), ((), ())), preferred_element_type=jnp.float32
    )


def contract_cols(left_matrix, right_matrix):
    return lax.dot_general(
        left_matrix, right_matrix, (((1,), (1,)), ((), ())), preferred_element_type=jnp.float32
    )


def layer_norm(field, gain, shift):
    center = field - jnp.mean(field, axis=-1, keepdims=True)
    spread = jnp.mean(center * center, axis=-1, keepdims=True)
    return center * lax.rsqrt(spread + ln_eps) * gain + shift


def gelu_exact(field):
    return jax.nn.gelu(field, approximate=False)


def rotate(field, places, rot_dims):
    half_dims = rot_dims // 2
    frequency = 10000.0 ** (-2.0 * jnp.arange(half_dims, dtype=jnp.float32) / rot_dims)
    angles = places.astype(jnp.float32)[:, None] * frequency[None, :]
    cosine = jnp.cos(angles)[:, None, :]
    sine_part = jnp.sin(angles)[:, None, :]
    front = field[..., :half_dims]
    middle = field[..., half_dims:rot_dims]
    return jnp.concatenate(
        [
            front * cosine - middle * sine_part,
            middle * cosine + front * sine_part,
            field[..., rot_dims:],
        ],
        axis=-1,
    )


def row_places(first_len, second_len, part_index, local_index, part_count):
    first_rows = first_len // part_count
    in_first = local_index < first_rows
    segment = jnp.where(in_first, 0, 1).astype(jnp.int32)
    position = jnp.where(
        in_first,
        part_index * first_rows + local_index,
        part_index * (second_len // part_count) + local_index - first_rows,
    )
    return (segment, position)


def soap_block(gradient, weight, first_moment, second_moment, left_basis, right_basis, step_rate):
    turned = exact_dot(exact_dot(left_basis.T, gradient), right_basis)
    first_new = beta_one * first_moment + (1.0 - beta_one) * turned
    second_new = beta_two * second_moment + (1.0 - beta_two) * turned * turned
    direction = (
        first_new
        / (1.0 - beta_one**STEP)
        / (jnp.sqrt(second_new / (1.0 - beta_two**STEP)) + adam_eps)
    )
    returned = exact_dot(exact_dot(left_basis, direction), right_basis.T)
    return (weight * (1.0 - step_rate * weight_decay) - step_rate * returned, first_new, second_new)


def adam_vector(gradient, current, first_moment, second_moment):
    first_new = beta_one * first_moment + (1.0 - beta_one) * gradient
    second_new = beta_two * second_moment + (1.0 - beta_two) * gradient * gradient
    direction = (
        first_new
        / (1.0 - beta_one**STEP)
        / (jnp.sqrt(second_new / (1.0 - beta_two**STEP)) + adam_eps)
    )
    return (current - rate_vector * direction, first_new, second_new)


UP = [(i, (i + 1) % 4) for i in range(4)]
DOWN = [(i, (i + 3) % 4) for i in range(4)]
PAIR = [(0, 1), (1, 0)]
GROUP_AXES = ("y", "c", "s")
bf16 = jnp.bfloat16
f32 = jnp.float32
ROWS = 1024
TILE = 256
ANY = pl.BlockSpec(memory_space=pl.ANY)
SCALARS = pl.BlockSpec(memory_space=pltpu.SMEM)
NN = (((1,), (0,)), ((), ()))
NT = (((1,), (1,)), ((), ()))
TN = (((0,), (0,)), ((), ()))


def mxu(left_matrix, right_matrix, dims):
    return lax.dot_general(left_matrix, right_matrix, dims, preferred_element_type=f32)


def wide(values):
    return values.astype(f32)


def low(values):
    return values.astype(bf16)


def struct(shape, dtype):
    return jax.ShapeDtypeStruct(shape, dtype)


def tiled(rows, columns):
    return pl.BlockSpec((rows, columns), lambda i: (i, 0))


def whole(*shape):
    return pl.BlockSpec(shape, lambda i: (0,) * len(shape))


def run(kernel, steps, ins, in_specs, outs, out_specs, scratch, flops, moved):
    return pl.pallas_call(
        kernel,
        name=kernel.__name__,
        grid=(steps,),
        in_specs=in_specs,
        out_specs=out_specs,
        out_shape=outs,
        scratch_shapes=scratch,
        compiler_params=pltpu.CompilerParams(vmem_limit_bytes=60 * 2**20),
        cost_estimate=pl.CostEstimate(flops=flops, bytes_accessed=moved, transcendentals=0),
    )(*ins)


def group_slots():
    y, c, s = lax.axis_index("y"), lax.axis_index("c"), lax.axis_index("s")
    r = jnp.arange(16, dtype=jnp.int32)
    core = c ^ (r // 8)
    row = (y + (r // 2) % 4) % 4
    part = s ^ (r % 2)
    return (row * 2 + core) * 2 + part


def load_rows(places, which, near, far, width, target, sems):
    copies = []
    for r in range(16):
        origin = (near if r < 8 else far).at[r % 8, :, pl.ds(0, width)]
        start = pl.multiple_of(places[which, r] * 128, 128)
        copies.append(pltpu.make_async_copy(origin, target.at[pl.ds(start, 128)], sems.at[r]))
    return copies


def load_hidden(order, which, blocks, target, sems):
    copies = []
    for j in range(16):
        start = pl.multiple_of(order[which, j] * 128, 128)
        origin = blocks.at[j]
        copies.append(pltpu.make_async_copy(origin, target.at[pl.ds(start, 128)], sems.at[j]))
    return copies


def load_out(places, near, far, target, sems):
    copies = []
    for r in range(16):
        for half in range(2):
            origin = (near if r < 8 else far).at[r % 8, :, pl.ds(768 + half * 128, 128)]
            start = pl.multiple_of(places[1, r] * 128, 128)
            copies.append(
                pltpu.make_async_copy(
                    origin,
                    target.at[pl.ds(half * 128, 128), pl.ds(start, 128)],
                    sems.at[r * 2 + half],
                )
            )
    return copies


def at_first(copies):
    @pl.when(pl.program_id(0) == 0)
    def _():
        for copy in copies:
            copy.start()
        for copy in copies:
            copy.wait()


def norm_kernel(x_ref, vec_ref, one_ref, two_ref, one_flip, two_flip, mean_ref, inverse_ref):
    field = wide(x_ref[...])
    mean = jnp.mean(field, axis=-1, keepdims=True)
    center = field - mean
    inverse = lax.rsqrt(jnp.mean(center * center, axis=-1, keepdims=True) + ln_eps)
    unit = center * inverse
    one = low(unit * vec_ref[0:1, :] + vec_ref[1:2, :])
    two = low(unit * vec_ref[2:3, :] + vec_ref[3:4, :])
    one_ref[...] = one
    two_ref[...] = two
    one_flip[...] = one.T
    two_flip[...] = two.T
    mean_ref[...] = mean
    inverse_ref[...] = inverse


def place_kernel(places, order, near, far, blocks, out_ref, up_ref, w_out, w_up, sems, more, last):
    first = load_out(places, near, far, w_out, sems)
    second = load_hidden(order, 0, blocks, w_up, more)
    for copy in first + second:
        copy.start()
    for copy in first:
        copy.wait()
    one = pltpu.make_async_copy(w_out, out_ref, last.at[0])
    one.start()
    for copy in second:
        copy.wait()
    two = pltpu.make_async_copy(w_up, up_ref, last.at[1])
    two.start()
    one.wait()
    two.wait()


def place_down_kernel(order, blocks, down_ref, w_down, sems, last):
    copies = load_hidden(order, 1, blocks, w_down, sems)
    for copy in copies:
        copy.start()
    for copy in copies:
        copy.wait()
    out = pltpu.make_async_copy(w_down, down_ref, last)
    out.start()
    out.wait()


def turn(field, table, way):
    head = field[:, :128]
    lane = lax.broadcasted_iota(jnp.int32, (1, 128), 1)
    cosine = jnp.where(lane < 64, table, 1.0)
    sine = jnp.where(lane < 64, pltpu.roll(table, 64, 1), 0.0)
    moved = jnp.where(lane < 32, pltpu.roll(head, 96, 1), pltpu.roll(head, 32, 1)) * sine
    return jnp.concatenate([head * cosine + way * moved, field[:, 128:]], axis=1)


def qkv_kernel(
    places, h_ref, near, far, bias_ref, table_ref, q_ref, k_ref, v_ref, w_ref, weight, sems, last
):
    at_first(load_rows(places, 0, near, far, 768, weight, sems))
    keep = pltpu.make_async_copy(weight, w_ref, last)

    @pl.when(pl.program_id(0) == 0)
    def _():
        keep.start()

    raw = mxu(h_ref[...], weight[...], NN) + bias_ref[...]
    table = table_ref[...]
    q_ref[...] = low(turn(raw[:, :256], table, 1.0))
    k_ref[...] = low(turn(raw[:, 256:512], table, 1.0))
    v_ref[...] = low(raw[:, 512:])

    @pl.when(pl.program_id(0) == pl.num_programs(0) - 1)
    def _():
        keep.wait()


def up_kernel(h_ref, w_ref, bias_ref, hidden_ref, slope_ref, flip_ref):
    pre = mxu(h_ref[...], w_ref[...], NN) + bias_ref[...]
    share = 0.5 * (1.0 + lax.erf(pre * 0.7071067811865476))
    hidden = low(pre * share)
    hidden_ref[...] = hidden
    flip_ref[...] = hidden.T
    slope_ref[...] = share + pre * (jnp.exp(-0.5 * pre * pre) * 0.3989422804014327)


def attention_kernel(
    lens,
    q_ref,
    k_ref,
    v_ref,
    fk_ref,
    fv_ref,
    dy_ref,
    w_ref,
    table_ref,
    att_ref,
    flip_ref,
    dq_ref,
    dkv_ref,
    dfk_ref,
    dfv_ref,
    flipped,
    total,
):
    step = pl.program_id(0)
    scale = 0.0625

    @pl.when(step == 0)
    def _():
        for part, refs in enumerate(((k_ref, v_ref), (fk_ref, fv_ref))):
            for which in range(2):
                flipped[which, :, pl.ds(part * ROWS, ROWS)] = refs[which][...].T
        total[...] = jnp.zeros_like(total)

    first, second, part = lens[0], lens[1], lens[2]

    def tile(extent):
        query = low(wide(q_ref[...]) * scale)
        q_index = lax.broadcasted_iota(jnp.int32, (1, TILE), 1) + (extent - TILE)
        q_seg = jnp.where(q_index < first, 0, 1)
        q_pos = jnp.where(q_index < first, first + q_index, second + q_index - first)

        k_index = lax.broadcasted_iota(jnp.int32, (extent, 1), 0)
        own_seen = (jnp.where(k_index < first, 0, 1) == q_seg) & (k_index <= q_index)
        f_index = lax.broadcasted_iota(jnp.int32, (ROWS, 1), 0)
        f_seg = jnp.where(part == 1, jnp.where(f_index < first, 0, 1), 2)
        f_pos = jnp.where(f_index < first, f_index, f_index - first)
        far_seen = (f_seg == q_seg) & (f_pos <= q_pos)

        own = jnp.where(own_seen, mxu(k_ref[:extent], query, NT), -1e30)
        other = jnp.where(far_seen, mxu(fk_ref[...], query, NT), -1e30)
        grad = low(mxu(dy_ref[...], w_ref[...], NT))
        top = jnp.maximum(
            jnp.max(own, axis=0, keepdims=True), jnp.max(other, axis=0, keepdims=True)
        )
        own = jnp.exp(own - top)
        other = jnp.exp(other - top)
        bottom = 1.0 / (
            jnp.sum(own, axis=0, keepdims=True) + jnp.sum(other, axis=0, keepdims=True)
        )
        own = own * bottom
        other = other * bottom
        own_low, other_low = low(own), low(other)
        own_grad = mxu(v_ref[:extent], grad, NT)
        other_grad = mxu(fv_ref[...], grad, NT)
        attended = mxu(flipped[1, :, :extent], own_low, NN) + mxu(
            flipped[1, :, ROWS:], other_low, NN
        )
        flip_ref[...] = low(attended)
        att_ref[...] = low(attended.T)
        total[1, :extent] += mxu(own_low, grad, NN)
        total[1, ROWS:] += mxu(other_low, grad, NN)
        inner = jnp.sum(own * own_grad, axis=0, keepdims=True) + jnp.sum(
            other * other_grad, axis=0, keepdims=True
        )
        own_low = low(own * (own_grad - inner))
        other_low = low(other * (other_grad - inner))
        total[0, :extent] += mxu(own_low, query, NN)
        total[0, ROWS:] += mxu(other_low, query, NN)
        turned_grad = mxu(flipped[0, :, :extent], own_low, NN) + mxu(
            flipped[0, :, ROWS:], other_low, NN
        )
        dq_ref[...] = low(turn(turned_grad.T * scale, table_ref[...], -1.0))

    for number in range(ROWS // TILE):

        @pl.when(step == number)
        def _():
            tile((number + 1) * TILE)

    @pl.when(step == pl.num_programs(0) - 1)
    def _():
        dkv_ref[...] = total[:, :ROWS]
        dfk_ref[...] = low(total[0, ROWS:])
        dfv_ref[...] = low(total[1, ROWS:])


def finish_kernel(dq_ref, dkv_ref, fk_ref, fv_ref, table_ref, out_ref):
    out_ref[:, :256] = dq_ref[...]
    out_ref[:, 256:512] = low(turn(dkv_ref[0] + wide(fk_ref[...]), table_ref[...], -1.0))
    out_ref[:, 512:] = low(dkv_ref[1] + wide(fv_ref[...]))


def branch_kernel(att_ref, hidden_ref, out_w, down_w, out_ref):
    out_ref[...] = low(mxu(att_ref[...], out_w[...], NN) + mxu(hidden_ref[...], down_w[...], NT))


def slope_kernel(dy_ref, down_w, slope_ref, out_ref):
    out_ref[...] = low(mxu(dy_ref[...], down_w[...], NN) * slope_ref[...])


def unit_kernel(
    first, x_ref, mean_ref, inverse_ref, dqkv_ref, dpre_ref, vec_ref, bias_ref, w_qkv, w_up,
    out_1, out_2, out_3, out_0, sum_ref, result, split_ref,
):
    step = pl.program_id(0)

    @pl.when(step == 0)
    def _():
        split_ref[:, :768] = jnp.sum(wide(dqkv_ref[...]), axis=0, keepdims=True)
        split_ref[:, 768:1792] = jnp.sum(wide(dpre_ref[...]), axis=0, keepdims=True)
        split_ref[:, 1792:] = jnp.zeros((1, 256), f32)

    unit = (wide(x_ref[...]) - mean_ref[...]) * inverse_ref[...]
    one = mxu(dqkv_ref[...], w_qkv[...], NT)
    two = mxu(dpre_ref[...], w_up[...], NT)
    result[...] = low(one * vec_ref[0:1, :] + two * vec_ref[2:3, :])
    sum_ref[0:1, :] = jnp.sum(one * unit, axis=0, keepdims=True)
    sum_ref[1:2, :] = jnp.sum(one, axis=0, keepdims=True)
    sum_ref[2:3, :] = jnp.sum(two * unit, axis=0, keepdims=True)
    sum_ref[3:4, :] = jnp.sum(two, axis=0, keepdims=True)
    sum_ref[4:5, :] = bias_ref[...]
    sum_ref[5:6, :] = split_ref[:, pl.ds(pl.multiple_of(step * 512, 512), 512)]
    sum_ref[6:8, :] = jnp.zeros((2, 512), f32)
    for number, ref in enumerate((out_1, out_2, out_3, out_0)):
        start = pl.multiple_of((first[0] + number) % 4 * 256, 256)
        ref[...] = result[pl.ds(start, 256), :]


def column_grads_kernel(places, att_ref, hidden_ref, d0, d1, d2, d3, o0, o1, o2, o3, far_ref, near_ref):
    step = pl.program_id(0)
    down = low(
        mxu(hidden_ref[...], jnp.concatenate([d0[...], d1[...], d2[...], d3[...]], axis=1), NN)
    )
    out = low(mxu(att_ref[...], jnp.concatenate([o0[...], o1[...], o2[...], o3[...]], axis=1), NN))
    for when, ref in ((step < 2, far_ref), (step >= 2, near_ref)):

        @pl.when(when)
        def _():
            for k in range(4):
                ref[k, :1024] = down[:, k * 128 : k * 128 + 128]
                ref[k, 1024:] = out[:, k * 128 : k * 128 + 128]


def row_grads_kernel(places, a0, a1, a2, a3, b0, b1, b2, b3, dqkv_ref, dpre_ref, far_ref, near_ref):
    step = pl.program_id(0)
    qkv = low(mxu(jnp.concatenate([a0[...], a1[...], a2[...], a3[...]], axis=0), dqkv_ref[...], NN))
    up = low(mxu(jnp.concatenate([b0[...], b1[...], b2[...], b3[...]], axis=0), dpre_ref[...], NN))
    for when, ref in ((step < 2, far_ref), (step >= 2, near_ref)):

        @pl.when(when)
        def _():
            for k in range(4):
                ref[k, :, :768] = qkv[k * 128 : k * 128 + 128]
                ref[k, :, 768:] = up[k * 128 : k * 128 + 128]


def fixed(*shape):
    return pl.BlockSpec(shape, lambda i, *_: (0,) * len(shape))


def led(kernel, steps, lead, ins, in_specs, outs, out_specs, scratch, flops, moved):
    return pl.pallas_call(
        kernel,
        name=kernel.__name__,
        grid_spec=pltpu.PrefetchScalarGridSpec(
            num_scalar_prefetch=1,
            grid=(steps,),
            in_specs=in_specs,
            out_specs=out_specs,
            scratch_shapes=scratch,
        ),
        out_shape=outs,
        compiler_params=pltpu.CompilerParams(vmem_limit_bytes=60 * 2**20),
        cost_estimate=pl.CostEstimate(flops=flops, bytes_accessed=moved, transcendentals=0),
    )(lead, *ins)


def run_norm(tokens, shared_vec):
    return run(
        norm_kernel,
        4,
        (tokens, shared_vec),
        [tiled(256, 2048), whole(6, 2048)],
        [struct((ROWS, 2048), bf16)] * 2
        + [struct((2048, ROWS), bf16)] * 2
        + [struct((ROWS, 1), f32)] * 2,
        [tiled(256, 2048)] * 2
        + [pl.BlockSpec((2048, 256), lambda i: (0, i))] * 2
        + [tiled(256, 1)] * 2,
        [],
        2**24,
        20 * 2**20,
    )


def run_qkv(places, h_one, near, far, bias, table):
    return run(
        qkv_kernel,
        ROWS // TILE,
        (places, h_one, near, far, bias, table),
        [SCALARS, tiled(TILE, 2048), ANY, ANY, whole(1, 768), tiled(TILE, 128)],
        [struct((ROWS, 256), bf16)] * 3 + [struct((2048, 768), bf16)],
        [tiled(TILE, 256)] * 3 + [ANY],
        [pltpu.VMEM((2048, 768), bf16), pltpu.SemaphoreType.DMA((16,)), pltpu.SemaphoreType.DMA],
        2 * ROWS * 2048 * 768,
        9 * 2**20,
    )


def run_place(places, order, near, far, blocks):
    dma = pltpu.SemaphoreType.DMA
    shapes = ((256, 2048), (2048, 1024))
    return run(
        place_kernel,
        1,
        (places, order, near, far, blocks),
        [SCALARS, SCALARS, ANY, ANY, ANY],
        [struct(shape, bf16) for shape in shapes],
        [ANY] * 2,
        [pltpu.VMEM(shape, bf16) for shape in shapes] + [dma((32,)), dma((16,)), dma((2,))],
        1,
        10 * 2**20,
    )


def run_place_down(order, blocks):
    dma = pltpu.SemaphoreType.DMA
    return run(
        place_down_kernel,
        1,
        (order, blocks),
        [SCALARS, ANY],
        struct((2048, 1024), bf16),
        ANY,
        [pltpu.VMEM((2048, 1024), bf16), dma((16,)), dma],
        1,
        8 * 2**20,
    )


def run_up(h_two, w_up, bias):
    return run(
        up_kernel,
        ROWS // TILE,
        (h_two, w_up, bias),
        [tiled(TILE, 2048), whole(2048, 1024), whole(1, 1024)],
        [struct((ROWS, 1024), bf16), struct((ROWS, 1024), f32), struct((1024, ROWS), bf16)],
        [tiled(TILE, 1024)] * 2 + [pl.BlockSpec((1024, TILE), lambda i: (0, i))],
        [],
        2 * ROWS * 2048 * 1024,
        16 * 2**20,
    )


def run_attention(lens, query, key, value, far_key, far_value, cotangent, w_out, table):
    return run(
        attention_kernel,
        ROWS // TILE,
        (lens, query, key, value, far_key, far_value, cotangent, w_out, table),
        [SCALARS, tiled(TILE, 256)]
        + [whole(ROWS, 256)] * 4
        + [tiled(TILE, 2048), whole(256, 2048), tiled(TILE, 128)],
        [struct((ROWS, 256), bf16), struct((256, ROWS), bf16), struct((ROWS, 256), bf16)]
        + [struct((2, ROWS, 256), f32)]
        + [struct((ROWS, 256), bf16)] * 2,
        [tiled(TILE, 256), pl.BlockSpec((256, TILE), lambda i: (0, i)), tiled(TILE, 256)]
        + [whole(2, ROWS, 256)]
        + [whole(ROWS, 256)] * 2,
        [pltpu.VMEM((2, 256, 2 * ROWS), bf16), pltpu.VMEM((2, 2 * ROWS, 256), f32)],
        8 * 2**30,
        12 * 2**20,
    )


def run_branch(attended, hidden, w_out, w_down):
    return run(
        branch_kernel,
        ROWS // TILE,
        (attended, hidden, w_out, w_down),
        [tiled(TILE, 256), tiled(TILE, 1024), whole(256, 2048), whole(2048, 1024)],
        struct((ROWS, 2048), bf16),
        tiled(TILE, 2048),
        [],
        2 * ROWS * 2048 * 1280,
        12 * 2**20,
    )


def run_slope(cotangent, w_down, slope):
    return run(
        slope_kernel,
        ROWS // TILE,
        (cotangent, w_down, slope),
        [tiled(TILE, 2048), whole(2048, 1024), tiled(TILE, 1024)],
        struct((ROWS, 1024), bf16),
        tiled(TILE, 1024),
        [],
        2 * ROWS * 2048 * 1024,
        14 * 2**20,
    )


def run_finish(grad_query, grad_kv, far_gkey, far_gvalue, table):
    kv_spec = pl.BlockSpec((2, 512, 256), lambda i: (0, i, 0))
    return run(
        finish_kernel,
        2,
        (grad_query, grad_kv, far_gkey, far_gvalue, table),
        [tiled(512, 256), kv_spec] + [tiled(512, 256)] * 2 + [tiled(512, 128)],
        struct((ROWS, 768), bf16),
        tiled(512, 768),
        [],
        2**20,
        6 * 2**20,
    )


def run_unit(first, tokens, mean, inverse, grad_qkv, grad_pre, shared_vec, bias_sum, w_qkv, w_up):
    def chunk(rows):
        return pl.BlockSpec((rows, 512), lambda i, lead: (0, i))

    return led(
        unit_kernel,
        4,
        first,
        (tokens, mean, inverse, grad_qkv, grad_pre, shared_vec, bias_sum, w_qkv, w_up),
        [chunk(ROWS), fixed(ROWS, 1), fixed(ROWS, 1), fixed(ROWS, 768), fixed(ROWS, 1024), chunk(6), chunk(1)]
        + [pl.BlockSpec((512, width), lambda i, lead: (i, 0)) for width in (768, 1024)],
        [struct((256, 2048), bf16)] * 4 + [struct((8, 2048), f32)],
        [chunk(256)] * 4 + [chunk(8)],
        [pltpu.VMEM((ROWS, 512), bf16), pltpu.VMEM((1, 2048), f32)],
        2 * ROWS * 2048 * 1792,
        20 * 2**20,
    )


def run_column_grads(places, att_flip, hidden_flip, cotangent):
    def block(which, k):
        return pl.BlockSpec((ROWS, 128), lambda i, p: (0, p[which, (i * 4 + 8 + k) % 16]))

    return led(
        column_grads_kernel,
        4,
        places,
        (att_flip, hidden_flip) + (cotangent,) * 8,
        [fixed(256, ROWS), fixed(1024, ROWS)]
        + [block(3, k) for k in range(4)]
        + [block(1, k) for k in range(4)],
        [struct((8, 1280, 128), bf16)] * 2,
        [
            pl.BlockSpec((4, 1280, 128), lambda i, p: (jnp.minimum(i, 1), 0, 0)),
            pl.BlockSpec((4, 1280, 128), lambda i, p: (jnp.maximum(i - 2, 0), 0, 0)),
        ],
        [],
        2 * ROWS * 2048 * 1280,
        12 * 2**20,
    )


def run_row_grads(places, one_flip, two_flip, grad_qkv, grad_pre):
    def block(which, k):
        return pl.BlockSpec((128, ROWS), lambda i, p: (p[which, (i * 4 + 8 + k) % 16], 0))

    return led(
        row_grads_kernel,
        4,
        places,
        (one_flip,) * 4 + (two_flip,) * 4 + (grad_qkv, grad_pre),
        [block(0, k) for k in range(4)]
        + [block(2, k) for k in range(4)]
        + [fixed(ROWS, 768), fixed(ROWS, 1024)],
        [struct((8, 128, 1792), bf16)] * 2,
        [
            pl.BlockSpec((4, 128, 1792), lambda i, p: (jnp.minimum(i, 1), 0, 0)),
            pl.BlockSpec((4, 128, 1792), lambda i, p: (jnp.maximum(i - 2, 0), 0, 0)),
        ],
        [],
        2 * ROWS * 2048 * 1792,
        16 * 2**20,
    )


def lay_kernel(starts, *refs):
    ins, out, hold, in_sems, out_sems = refs[:-4], refs[-4], refs[-3], refs[-2], refs[-1]
    inward, outward = [], []
    low = 0
    for k, ref in enumerate(ins):
        size = ref.shape[0]
        spot = hold.at[pl.ds(low, size)]
        low += size
        target = out.at[pl.ds(pl.multiple_of(starts[k] * 128, 128), size)]
        inward.append(pltpu.make_async_copy(ref, spot, in_sems.at[k]))
        outward.append(pltpu.make_async_copy(spot, target, out_sems.at[k]))
    for copy in inward:
        copy.start()
    for first, second in zip(inward, outward):
        first.wait()
        second.start()
    for copy in outward:
        copy.wait()


def copy_kernel(source, out, hold_ref, in_sems, out_sems):
    inward, outward = [], []
    for k in range(8):
        spot = pl.ds(k * 128, 128)
        inward.append(pltpu.make_async_copy(source.at[spot], hold_ref.at[spot], in_sems.at[k]))
        outward.append(pltpu.make_async_copy(hold_ref.at[spot], out.at[spot], out_sems.at[k]))
    for copy in inward:
        copy.start()
    for first, second in zip(inward, outward):
        first.wait()
        second.start()
    for copy in outward:
        copy.wait()


def copy_rows(field):
    return pl.pallas_call(
        copy_kernel,
        name="copy_kernel",
        out_shape=struct(field.shape, field.dtype),
        in_specs=[ANY],
        out_specs=ANY,
        scratch_shapes=[
            pltpu.VMEM(field.shape, field.dtype),
            pltpu.SemaphoreType.DMA((8,)),
            pltpu.SemaphoreType.DMA((8,)),
        ],
        compiler_params=pltpu.CompilerParams(vmem_limit_bytes=32 * 2**20),
    )(field)


def lay_rows(x, pieces):
    far = ((x + 2) % 4) * 2
    starts = jnp.stack([x * 2, ((x + 1) % 4) * 2, far, far + 1, ((x + 3) % 4) * 2])
    width, dtype = pieces[0].shape[1], pieces[0].dtype
    return pl.pallas_call(
        lay_kernel,
        name="lay_kernel",
        out_shape=struct((ROWS, width), dtype),
        in_specs=[SCALARS] + [ANY] * 5,
        out_specs=ANY,
        scratch_shapes=[
            pltpu.VMEM((ROWS, width), dtype),
            pltpu.SemaphoreType.DMA((5,)),
            pltpu.SemaphoreType.DMA((5,)),
        ],
        compiler_params=pltpu.CompilerParams(vmem_limit_bytes=32 * 2**20),
    )(starts, *pieces)


def up_y(values):
    return lax.ppermute(values, "y", UP)


def down_y(values):
    return lax.ppermute(values, "y", DOWN)


def up_x(values):
    return lax.ppermute(values, "x", UP)


def down_x(values):
    return lax.ppermute(values, "x", DOWN)


def swap(values, axis):
    return lax.ppermute(values, axis, PAIR)


def hold(values):
    return lax.optimization_barrier(values)


def join(*parts):
    return jnp.concatenate(parts, axis=0)


def soap_moments(gradient, first_moment, second_moment, left_basis, right_basis):
    turned = exact_dot(exact_dot(left_basis.T, gradient), right_basis)
    first_new = beta_one * first_moment + (1.0 - beta_one) * turned
    second_new = beta_two * second_moment + (1.0 - beta_two) * turned * turned
    direction = (
        first_new
        / (1.0 - beta_one**STEP)
        / (jnp.sqrt(second_new / (1.0 - beta_two**STEP)) + adam_eps)
    )
    return (exact_dot(left_basis, direction), first_new, second_new)


def soap_weight(state, weight, left_basis, right_basis, step_rate):
    returned = exact_dot(state[0], right_basis.T)
    return (weight * (1.0 - step_rate * weight_decay) - step_rate * returned, state[1], state[2])


def per_device(
    tokens,
    cotangent,
    seq_lens,
    owners,
    shared_vec,
    shared_first,
    shared_second,
    split_vec,
    split_first,
    split_second,
    qkv_master,
    qkv_first,
    qkv_second,
    qkv_left,
    qkv_right,
    out_master,
    out_first,
    out_second,
    out_left,
    out_right,
    up_master,
    up_first,
    up_second,
    up_left,
    up_right,
    down_master,
    down_first,
    down_second,
    down_left,
    down_right,
):
    part = lax.axis_index("s")
    x, z = lax.axis_index("x"), lax.axis_index("z")

    out_block = out_master.reshape(256, 128)
    packed = low(jnp.concatenate([qkv_master[0], out_block[:128], out_block[128:]], axis=1))[None]
    partner = swap(packed, "s")
    up_blocks = lax.all_gather(low(up_master), GROUP_AXES, axis=0, tiled=True)
    down_own = low(down_master.reshape(1024, 128).T)[None]
    lens = jnp.stack([seq_lens[0, 0] // 2, seq_lens[0, 1] // 2, part.astype(jnp.int32)])
    local_index = jnp.arange(ROWS, dtype=jnp.int32)
    _, position = row_places(seq_lens[0, 0], seq_lens[0, 1], part, local_index, 2)
    partner, tokens, lens, position = hold((partner, tokens, lens, position))
    h_one, h_two, one_flip, two_flip, mean, inverse = run_norm(tokens, shared_vec)
    bias_sum = jnp.sum(wide(cotangent), axis=0, keepdims=True) * 0.125
    pair = join(packed, partner)
    before, after = up_y(pair), down_y(pair)
    slots = group_slots()
    ids = jnp.arange(16, dtype=jnp.int32)
    places = jnp.sum(
        jnp.where(owners[:, None, :] == slots[None, :, None], ids[None, None, :], 0), axis=2
    )
    order = jnp.sum(jnp.where(owners[2:, None, :] == ids[None, :, None], ids, 0), axis=2)
    frequency = 10000.0 ** (-2.0 * jnp.arange(32, dtype=f32) / 64)
    angles = position.astype(f32)[:, None] * frequency[None, :]
    cosine, sine_part = jnp.cos(angles), jnp.sin(angles)
    table = jnp.concatenate([cosine, cosine, -sine_part, sine_part], axis=1)
    bias_qkv, bias_up = split_vec[:, :768], split_vec[:, 768:]

    (
        before, after, h_one, h_two, one_flip, two_flip, mean, inverse, places, order, lens, table, bias_qkv, bias_up, bias_sum,
    ) = hold((
        before, after, h_one, h_two, one_flip, two_flip, mean, inverse, places, order, lens, table, bias_qkv, bias_up, bias_sum,
    ))
    far_a, far_b = up_y(before[0:1]), down_y(after[1:2])
    far_a, far_b = hold((far_a, far_b))
    near = join(pair, after, far_a, far_b, before)
    far = swap(near, "c")
    query, key, value, w_qkv = run_qkv(places, h_one, near, far, bias_qkv, table)
    far_key = lax.ppermute(key, "s", [(0, 1)])
    far_value = lax.ppermute(value, "s", [(0, 1)])
    up_blocks, down_own, h_two, query = hold((up_blocks, down_own, h_two, query))
    down_blocks = lax.all_gather(down_own, GROUP_AXES, axis=0, tiled=True)
    w_out, w_up = run_place(places, order, near, far, up_blocks)
    hidden, slope, hidden_flip = run_up(h_two, w_up, bias_up)
    far_key, far_value, hidden, slope, hidden_flip = hold(
        (far_key, far_value, hidden, slope, hidden_flip)
    )
    attended, att_flip, grad_query, grad_kv, far_gkey, far_gvalue = run_attention(
        lens, query, key, value, far_key, far_value, cotangent, w_out, table
    )
    attended, far_gkey, far_gvalue = hold((attended, far_gkey, far_gvalue))
    far_gkey = lax.ppermute(far_gkey, "s", [(1, 0)])
    far_gvalue = lax.ppermute(far_gvalue, "s", [(1, 0)])
    w_down = run_place_down(order, down_blocks)
    partial_out = run_branch(attended, hidden, w_out, w_down)
    partial_out, far_gkey, far_gvalue, slope = hold((partial_out, far_gkey, far_gvalue, slope))
    part_sum = lax.psum_scatter(partial_out, "x", scatter_dimension=0, tiled=True)
    grad_pre = run_slope(cotangent, w_down, slope)
    grad_pre, grad_query = hold((grad_pre, grad_query))
    grad_qkv = run_finish(grad_query, grad_kv, far_gkey, far_gvalue, table)
    row_far, row_near = run_row_grads(places, one_flip, two_flip, grad_qkv, grad_pre)
    row_far, row_near, grad_qkv, grad_pre = hold((row_far, row_near, grad_qkv, grad_pre))
    rows = (row_near, swap(row_far, "c"))

    def both(pair, start, stop):
        return wide(pair[0][start:stop]) + wide(pair[1][start:stop])

    def first_hop(pair):
        return up_y(low(both(pair, 4, 5))), down_y(low(both(pair, 5, 6)))

    def second_hop(pair, first, last):
        ahead = up_y(low(join(both(pair, 2, 3) + wide(first), both(pair, 3, 4))))
        behind = down_y(low(join(both(pair, 6, 7), both(pair, 7, 8) + wide(last))))
        return ahead, behind

    def last_hop(pair, ahead, behind):
        total = both(pair, 0, 2) + wide(ahead) + wide(behind)
        return total[0] + wide(swap(low(total[1]), "s"))

    unit_1, unit_2, unit_3, unit_0, sums = run_unit(
        jnp.stack([x + 1]).astype(jnp.int32),
        tokens,
        mean,
        inverse,
        grad_qkv,
        grad_pre,
        shared_vec,
        bias_sum,
        w_qkv,
        w_up,
    )

    def own(values_in):
        return wide(lax.dynamic_slice_in_dim(values_in, (x * 2 + z) * 128, 128, axis=0))

    def half(values, which):
        return lax.dynamic_slice_in_dim(values, which * 128, 128, axis=0)

    def both_rows(mine, theirs):
        return join(jnp.where(z == 0, mine, theirs), jnp.where(z == 0, theirs, mine))

    near_y = [(i, i ^ 1) for i in range(4)]
    far_y = [(i, i ^ 2) for i in range(4)]

    unit_1, unit_2, unit_3, unit_0, sums, rows, part_sum, hidden_flip = hold(
        (unit_1, unit_2, unit_3, unit_0, sums, rows, part_sum, hidden_flip)
    )
    unit_1, unit_3 = up_x(unit_1), down_x(unit_3)
    row_a, row_b = first_hop(rows)
    out_partner = swap(half(part_sum, 1 - z), "z")
    column_far, column_near = run_column_grads(places, att_flip, hidden_flip, cotangent)
    unit_1, unit_3, row_a, row_b, out_partner, sums, column_far, column_near = hold(
        (unit_1, unit_3, row_a, row_b, out_partner, sums, column_far, column_near)
    )
    unit_2 = lax.ppermute(unit_2, "x", far_y)
    row_prev, row_next = second_hop(rows, row_a, row_b)
    columns = (column_near, swap(column_far, "c"))
    out_rows = low(
        own(tokens) + wide(half(part_sum, z)) + wide(out_partner) + shared_vec[4] + shared_vec[5]
    )
    out_twin = swap(out_rows, "z")
    total = wide(unit_0) + wide(unit_1) + wide(unit_3)
    unit_2, total, row_prev, row_next, columns, out_rows, out_twin, sums = hold(
        (unit_2, total, row_prev, row_next, columns, out_rows, out_twin, sums)
    )
    output = lax.all_gather(both_rows(out_rows, out_twin), "x", axis=0, tiled=True)
    total = total + wide(unit_2)
    own_grad = half(total, z) + wide(swap(low(half(total, 1 - z)), "z"))
    row_sum = last_hop(rows, row_prev, row_next)
    column_a, column_b = first_hop(columns)
    sums = sums + swap(sums, "c")
    own_grad, row_sum, column_a, column_b, sums = hold(
        (own_grad, row_sum, column_a, column_b, sums)
    )
    own_inverse = lax.dynamic_slice_in_dim(inverse, (x * 2 + z) * 128, 128, axis=0)
    own_mean = lax.dynamic_slice_in_dim(mean, (x * 2 + z) * 128, 128, axis=0)
    own_unit = (own(tokens) - own_mean) * own_inverse
    grad_x = (
        own_grad
        - jnp.mean(own_grad, axis=-1, keepdims=True)
        - own_unit * jnp.mean(own_grad * own_unit, axis=-1, keepdims=True)
    ) * own_inverse
    grad_rows = low(own(cotangent) + grad_x)
    grad_twin = swap(grad_rows, "z")
    column_prev, column_next = second_hop(columns, column_a, column_b)
    sums = sums + swap(sums, "s")
    sums = sums + lax.ppermute(sums, "y", near_y)
    new_up = soap_block(
        row_sum[:, 768:], up_master[0], up_first[0], up_second[0], up_left[0, 0], up_right[0, 0], rate_up
    )
    grad_rows, grad_twin, row_sum, column_prev, column_next, sums, new_up = hold(
        (grad_rows, grad_twin, row_sum, column_prev, column_next, sums, new_up)
    )
    grad_pair = both_rows(grad_rows, grad_twin)
    grad_before, grad_after = up_x(grad_pair), down_x(grad_pair)
    column_sum = last_hop(columns, column_prev, column_next)
    sums = sums + lax.ppermute(sums, "y", far_y)
    shared_sum = sums + swap(sums, "z")
    new_qkv = soap_block(
        row_sum[:, :768],
        qkv_master[0],
        qkv_first[0],
        qkv_second[0],
        qkv_left[0, 0],
        qkv_right[0, 0],
        rate_qkv,
    )
    down_state = soap_moments(
        column_sum[:1024], down_first[:, 0], down_second[:, 0], down_left[0, 0], down_right[0, 0]
    )
    new_out = soap_block(
        column_sum[1024:],
        out_master[:, 0],
        out_first[:, 0],
        out_second[:, 0],
        out_left[0, 0],
        out_right[0, 0],
        rate_out,
    )
    grad_before, grad_after, grad_pair, shared_sum, new_qkv, new_out, down_state, output = hold(
        (grad_before, grad_after, grad_pair, shared_sum, new_qkv, new_out, down_state, output)
    )
    far_a, far_b = up_x(grad_before[:128]), down_x(grad_after[128:])
    shared_sum = shared_sum + lax.ppermute(shared_sum, "x", near_y)
    shared_sum = shared_sum + lax.ppermute(shared_sum, "x", far_y)
    output = copy_rows(output)
    new_down = soap_weight(
        down_state, down_master[:, 0], down_left[0, 0], down_right[0, 0], rate_down
    )
    far_a, far_b, shared_sum, output, new_down = hold(
        (far_a, far_b, shared_sum, output, new_down)
    )
    grad_input = lay_rows(x, [grad_pair, grad_after, far_a, far_b, grad_before])
    split_grad = sums[5:6, :1792]
    shared_grad = join(shared_sum[:5], shared_sum[4:5])
    new_shared = adam_vector(shared_grad, shared_vec, shared_first, shared_second)
    new_split = adam_vector(split_grad, split_vec, split_first, split_second)
    return (
        output,
        grad_input,
        new_shared[0],
        new_shared[1],
        new_shared[2],
        new_split[0],
        new_split[1],
        new_split[2],
        new_qkv[0][None],
        new_qkv[1][None],
        new_qkv[2][None],
        new_qkv[0][None].astype(bf16),
        new_out[0][:, None],
        new_out[1][:, None],
        new_out[2][:, None],
        new_out[0][:, None].astype(bf16),
        new_up[0][None],
        new_up[1][None],
        new_up[2][None],
        new_up[0][None].astype(bf16),
        new_down[0][:, None],
        new_down[1][:, None],
        new_down[2][:, None],
        new_down[0][:, None].astype(bf16),
    )


def solution(mesh):
    in_specs = (
        P(("y", "c", "s"), None),
        P(("y", "c", "s"), None),
        P(("y", "c"), None),
        P(),
        P(),
        P(),
        P(),
        P(("x", "z"), None),
        P(("x", "z"), None),
        P(("x", "z"), None),
        P(("y", "c", "s"), None, ("x", "z")),
        P(("y", "c", "s"), None, ("x", "z")),
        P(("y", "c", "s"), None, ("x", "z")),
        P(("y", "c", "s"), ("x", "z"), None, None),
        P(("y", "c", "s"), ("x", "z"), None, None),
        P(("x", "z"), ("y", "c", "s"), None),
        P(("x", "z"), ("y", "c", "s"), None),
        P(("x", "z"), ("y", "c", "s"), None),
        P(("y", "c", "s"), ("x", "z"), None, None),
        P(("y", "c", "s"), ("x", "z"), None, None),
        P(("y", "c", "s"), None, ("x", "z")),
        P(("y", "c", "s"), None, ("x", "z")),
        P(("y", "c", "s"), None, ("x", "z")),
        P(("y", "c", "s"), ("x", "z"), None, None),
        P(("y", "c", "s"), ("x", "z"), None, None),
        P(("x", "z"), ("y", "c", "s"), None),
        P(("x", "z"), ("y", "c", "s"), None),
        P(("x", "z"), ("y", "c", "s"), None),
        P(("y", "c", "s"), ("x", "z"), None, None),
        P(("y", "c", "s"), ("x", "z"), None, None),
    )
    out_specs = (
        P(("y", "c", "s"), None),
        P(("y", "c", "s"), None),
        P(),
        P(),
        P(),
        P(("x", "z"), None),
        P(("x", "z"), None),
        P(("x", "z"), None),
        P(("y", "c", "s"), None, ("x", "z")),
        P(("y", "c", "s"), None, ("x", "z")),
        P(("y", "c", "s"), None, ("x", "z")),
        P(("y", "c", "s"), None, ("x", "z")),
        P(("x", "z"), ("y", "c", "s"), None),
        P(("x", "z"), ("y", "c", "s"), None),
        P(("x", "z"), ("y", "c", "s"), None),
        P(("x", "z"), ("y", "c", "s"), None),
        P(("y", "c", "s"), None, ("x", "z")),
        P(("y", "c", "s"), None, ("x", "z")),
        P(("y", "c", "s"), None, ("x", "z")),
        P(("y", "c", "s"), None, ("x", "z")),
        P(("x", "z"), ("y", "c", "s"), None),
        P(("x", "z"), ("y", "c", "s"), None),
        P(("x", "z"), ("y", "c", "s"), None),
        P(("x", "z"), ("y", "c", "s"), None),
    )
    fine = Mesh(mesh.devices.reshape(4, 2, 2, 4, 2), ("y", "c", "s", "x", "z"))
    return jax.shard_map(
        per_device, mesh=fine, in_specs=in_specs, out_specs=out_specs, check_vma=False
    )
```

```python
import jax
import jax.numpy as jnp
from jax import lax
from jax.experimental import pallas as pl
from jax.experimental.pallas import tpu as pltpu
from jax.sharding import Mesh, PartitionSpec as P

D = 2048
H = 8
STEP = 5


ln_eps = 1e-05
adam_eps = 1e-08
beta_one = 0.5
beta_two = 0.5
rate_qkv = 0.01
rate_out = 0.05
rate_up = 0.01
rate_down = 0.005
rate_vector = 0.2
weight_decay = 0.01


def exact_dot(left_matrix, right_matrix):
    return jnp.dot(
        left_matrix,
        right_matrix,
        precision=lax.Precision.HIGH,
        preferred_element_type=jnp.float32,
    )


def contract_rows(left_matrix, right_matrix):
    return lax.dot_general(
        left_matrix, right_matrix, (((0,), (0,)), ((), ())), preferred_element_type=jnp.float32
    )


def contract_cols(left_matrix, right_matrix):
    return lax.dot_general(
        left_matrix, right_matrix, (((1,), (1,)), ((), ())), preferred_element_type=jnp.float32
    )


def layer_norm(field, gain, shift):
    center = field - jnp.mean(field, axis=-1, keepdims=True)
    spread = jnp.mean(center * center, axis=-1, keepdims=True)
    return center * lax.rsqrt(spread + ln_eps) * gain + shift


def gelu_exact(field):
    return jax.nn.gelu(field, approximate=False)


def rotate(field, places, rot_dims):
    half_dims = rot_dims // 2
    frequency = 10000.0 ** (-2.0 * jnp.arange(half_dims, dtype=jnp.float32) / rot_dims)
    angles = places.astype(jnp.float32)[:, None] * frequency[None, :]
    cosine = jnp.cos(angles)[:, None, :]
    sine_part = jnp.sin(angles)[:, None, :]
    front = field[..., :half_dims]
    middle = field[..., half_dims:rot_dims]
    return jnp.concatenate(
        [
            front * cosine - middle * sine_part,
            middle * cosine + front * sine_part,
            field[..., rot_dims:],
        ],
        axis=-1,
    )


def row_places(first_len, second_len, part_index, local_index, part_count):
    first_rows = first_len // part_count
    in_first = local_index < first_rows
    segment = jnp.where(in_first, 0, 1).astype(jnp.int32)
    position = jnp.where(
        in_first,
        part_index * first_rows + local_index,
        part_index * (second_len // part_count) + local_index - first_rows,
    )
    return (segment, position)


def soap_block(gradient, weight, first_moment, second_moment, left_basis, right_basis, step_rate):
    turned = exact_dot(exact_dot(left_basis.T, gradient), right_basis)
    first_new = beta_one * first_moment + (1.0 - beta_one) * turned
    second_new = beta_two * second_moment + (1.0 - beta_two) * turned * turned
    direction = (
        first_new
        / (1.0 - beta_one**STEP)
        / (jnp.sqrt(second_new / (1.0 - beta_two**STEP)) + adam_eps)
    )
    returned = exact_dot(exact_dot(left_basis, direction), right_basis.T)
    return (weight * (1.0 - step_rate * weight_decay) - step_rate * returned, first_new, second_new)


def adam_vector(gradient, current, first_moment, second_moment):
    first_new = beta_one * first_moment + (1.0 - beta_one) * gradient
    second_new = beta_two * second_moment + (1.0 - beta_two) * gradient * gradient
    direction = (
        first_new
        / (1.0 - beta_one**STEP)
        / (jnp.sqrt(second_new / (1.0 - beta_two**STEP)) + adam_eps)
    )
    return (current - rate_vector * direction, first_new, second_new)


UP = [(i, (i + 1) % 4) for i in range(4)]
DOWN = [(i, (i + 3) % 4) for i in range(4)]
PAIR = [(0, 1), (1, 0)]
GROUP_AXES = ("y", "c", "s")
bf16 = jnp.bfloat16
f32 = jnp.float32
ROWS = 1024
TILE = 256
ANY = pl.BlockSpec(memory_space=pl.ANY)
SCALARS = pl.BlockSpec(memory_space=pltpu.SMEM)
NN = (((1,), (0,)), ((), ()))
NT = (((1,), (1,)), ((), ()))
TN = (((0,), (0,)), ((), ()))


def mxu(left_matrix, right_matrix, dims):
    return lax.dot_general(left_matrix, right_matrix, dims, preferred_element_type=f32)


def wide(values):
    return values.astype(f32)


def low(values):
    return values.astype(bf16)


def struct(shape, dtype):
    return jax.ShapeDtypeStruct(shape, dtype)


def tiled(rows, columns):
    return pl.BlockSpec((rows, columns), lambda i: (i, 0))


def whole(*shape):
    return pl.BlockSpec(shape, lambda i: (0,) * len(shape))


def run(kernel, steps, ins, in_specs, outs, out_specs, scratch, flops, moved):
    return pl.pallas_call(
        kernel,
        name=kernel.__name__,
        grid=(steps,),
        in_specs=in_specs,
        out_specs=out_specs,
        out_shape=outs,
        scratch_shapes=scratch,
        compiler_params=pltpu.CompilerParams(vmem_limit_bytes=60 * 2**20),
        cost_estimate=pl.CostEstimate(flops=flops, bytes_accessed=moved, transcendentals=0),
    )(*ins)


def group_slots():
    y, c, s = lax.axis_index("y"), lax.axis_index("c"), lax.axis_index("s")
    r = jnp.arange(16, dtype=jnp.int32)
    core = c ^ (r // 8)
    row = (y + (r // 2) % 4) % 4
    part = s ^ (r % 2)
    return (row * 2 + core) * 2 + part


def load_rows(places, which, near, far, width, target, sems):
    copies = []
    for r in range(16):
        origin = (near if r < 8 else far).at[r % 8, :, pl.ds(0, width)]
        start = pl.multiple_of(places[which, r] * 128, 128)
        copies.append(pltpu.make_async_copy(origin, target.at[pl.ds(start, 128)], sems.at[r]))
    return copies


def load_hidden(order, which, blocks, target, sems):
    copies = []
    for j in range(16):
        start = pl.multiple_of(order[which, j] * 128, 128)
        origin = blocks.at[j]
        copies.append(pltpu.make_async_copy(origin, target.at[pl.ds(start, 128)], sems.at[j]))
    return copies


def load_out(places, near, far, target, sems):
    copies = []
    for r in range(16):
        for half in range(2):
            origin = (near if r < 8 else far).at[r % 8, :, pl.ds(768 + half * 128, 128)]
            start = pl.multiple_of(places[1, r] * 128, 128)
            copies.append(
                pltpu.make_async_copy(
                    origin,
                    target.at[pl.ds(half * 128, 128), pl.ds(start, 128)],
                    sems.at[r * 2 + half],
                )
            )
    return copies


def at_first(copies):
    @pl.when(pl.program_id(0) == 0)
    def _():
        for copy in copies:
            copy.start()
        for copy in copies:
            copy.wait()


def norm_kernel(x_ref, vec_ref, one_ref, two_ref, one_flip, two_flip, mean_ref, inverse_ref):
    field = wide(x_ref[...])
    mean = jnp.mean(field, axis=-1, keepdims=True)
    center = field - mean
    inverse = lax.rsqrt(jnp.mean(center * center, axis=-1, keepdims=True) + ln_eps)
    unit = center * inverse
    one = low(unit * vec_ref[0:1, :] + vec_ref[1:2, :])
    two = low(unit * vec_ref[2:3, :] + vec_ref[3:4, :])
    one_ref[...] = one
    two_ref[...] = two
    one_flip[...] = one.T
    two_flip[...] = two.T
    mean_ref[...] = mean
    inverse_ref[...] = inverse


def place_kernel(places, order, near, far, blocks, out_ref, up_ref, w_out, w_up, sems, more, last):
    first = load_out(places, near, far, w_out, sems)
    second = load_hidden(order, 0, blocks, w_up, more)
    for copy in first + second:
        copy.start()
    for copy in first:
        copy.wait()
    one = pltpu.make_async_copy(w_out, out_ref, last.at[0])
    one.start()
    for copy in second:
        copy.wait()
    two = pltpu.make_async_copy(w_up, up_ref, last.at[1])
    two.start()
    one.wait()
    two.wait()


def place_down_kernel(order, blocks, down_ref, w_down, sems, last):
    copies = load_hidden(order, 1, blocks, w_down, sems)
    for copy in copies:
        copy.start()
    for copy in copies:
        copy.wait()
    out = pltpu.make_async_copy(w_down, down_ref, last)
    out.start()
    out.wait()


def turn(field, table, way):
    head = field[:, :128]
    lane = lax.broadcasted_iota(jnp.int32, (1, 128), 1)
    cosine = jnp.where(lane < 64, table, 1.0)
    sine = jnp.where(lane < 64, pltpu.roll(table, 64, 1), 0.0)
    moved = jnp.where(lane < 32, pltpu.roll(head, 96, 1), pltpu.roll(head, 32, 1)) * sine
    return jnp.concatenate([head * cosine + way * moved, field[:, 128:]], axis=1)


def qkv_kernel(
    places, h_ref, near, far, bias_ref, table_ref, q_ref, k_ref, v_ref, w_ref, weight, sems, last
):
    at_first(load_rows(places, 0, near, far, 768, weight, sems))
    keep = pltpu.make_async_copy(weight, w_ref, last)

    @pl.when(pl.program_id(0) == 0)
    def _():
        keep.start()

    raw = mxu(h_ref[...], weight[...], NN) + bias_ref[...]
    table = table_ref[...]
    q_ref[...] = low(turn(raw[:, :256], table, 1.0))
    k_ref[...] = low(turn(raw[:, 256:512], table, 1.0))
    v_ref[...] = low(raw[:, 512:])

    @pl.when(pl.program_id(0) == pl.num_programs(0) - 1)
    def _():
        keep.wait()


def up_kernel(h_ref, w_ref, bias_ref, hidden_ref, slope_ref, flip_ref):
    pre = mxu(h_ref[...], w_ref[...], NN) + bias_ref[...]
    share = 0.5 * (1.0 + lax.erf(pre * 0.7071067811865476))
    hidden = low(pre * share)
    hidden_ref[...] = hidden
    flip_ref[...] = hidden.T
    slope_ref[...] = share + pre * (jnp.exp(-0.5 * pre * pre) * 0.3989422804014327)


def attention_kernel(
    lens,
    q_ref,
    k_ref,
    v_ref,
    fk_ref,
    fv_ref,
    dy_ref,
    w_ref,
    table_ref,
    att_ref,
    flip_ref,
    dq_ref,
    dkv_ref,
    dfk_ref,
    dfv_ref,
    flipped,
    total,
):
    step = pl.program_id(0)
    scale = 0.0625

    @pl.when(step == 0)
    def _():
        for part, refs in enumerate(((k_ref, v_ref), (fk_ref, fv_ref))):
            for which in range(2):
                flipped[which, :, pl.ds(part * ROWS, ROWS)] = refs[which][...].T
        total[...] = jnp.zeros_like(total)

    first, second, part = lens[0], lens[1], lens[2]

    def tile(extent):
        query = low(wide(q_ref[...]) * scale)
        q_index = lax.broadcasted_iota(jnp.int32, (1, TILE), 1) + (extent - TILE)
        q_seg = jnp.where(q_index < first, 0, 1)
        q_pos = jnp.where(q_index < first, first + q_index, second + q_index - first)

        k_index = lax.broadcasted_iota(jnp.int32, (extent, 1), 0)
        own_seen = (jnp.where(k_index < first, 0, 1) == q_seg) & (k_index <= q_index)
        f_index = lax.broadcasted_iota(jnp.int32, (ROWS, 1), 0)
        f_seg = jnp.where(part == 1, jnp.where(f_index < first, 0, 1), 2)
        f_pos = jnp.where(f_index < first, f_index, f_index - first)
        far_seen = (f_seg == q_seg) & (f_pos <= q_pos)

        own = jnp.where(own_seen, mxu(k_ref[:extent], query, NT), -1e30)
        other = jnp.where(far_seen, mxu(fk_ref[...], query, NT), -1e30)
        grad = low(mxu(dy_ref[...], w_ref[...], NT))
        top = jnp.maximum(
            jnp.max(own, axis=0, keepdims=True), jnp.max(other, axis=0, keepdims=True)
        )
        own = jnp.exp(own - top)
        other = jnp.exp(other - top)
        bottom = 1.0 / (
            jnp.sum(own, axis=0, keepdims=True) + jnp.sum(other, axis=0, keepdims=True)
        )
        own = own * bottom
        other = other * bottom
        own_low, other_low = low(own), low(other)
        own_grad = mxu(v_ref[:extent], grad, NT)
        other_grad = mxu(fv_ref[...], grad, NT)
        attended = mxu(flipped[1, :, :extent], own_low, NN) + mxu(
            flipped[1, :, ROWS:], other_low, NN
        )
        flip_ref[...] = low(attended)
        att_ref[...] = low(attended.T)
        total[1, :extent] += mxu(own_low, grad, NN)
        total[1, ROWS:] += mxu(other_low, grad, NN)
        inner = jnp.sum(own * own_grad, axis=0, keepdims=True) + jnp.sum(
            other * other_grad, axis=0, keepdims=True
        )
        own_low = low(own * (own_grad - inner))
        other_low = low(other * (other_grad - inner))
        total[0, :extent] += mxu(own_low, query, NN)
        total[0, ROWS:] += mxu(other_low, query, NN)
        turned_grad = mxu(flipped[0, :, :extent], own_low, NN) + mxu(
            flipped[0, :, ROWS:], other_low, NN
        )
        dq_ref[...] = low(turn(turned_grad.T * scale, table_ref[...], -1.0))

    for number in range(ROWS // TILE):

        @pl.when(step == number)
        def _():
            tile((number + 1) * TILE)

    @pl.when(step == pl.num_programs(0) - 1)
    def _():
        dkv_ref[...] = total[:, :ROWS]
        dfk_ref[...] = low(total[0, ROWS:])
        dfv_ref[...] = low(total[1, ROWS:])


def finish_kernel(dq_ref, dkv_ref, fk_ref, fv_ref, table_ref, out_ref):
    out_ref[:, :256] = dq_ref[...]
    out_ref[:, 256:512] = low(turn(dkv_ref[0] + wide(fk_ref[...]), table_ref[...], -1.0))
    out_ref[:, 512:] = low(dkv_ref[1] + wide(fv_ref[...]))


def branch_kernel(att_ref, hidden_ref, out_w, down_w, out_ref):
    out_ref[...] = low(mxu(att_ref[...], out_w[...], NN) + mxu(hidden_ref[...], down_w[...], NT))


def slope_kernel(dy_ref, down_w, slope_ref, out_ref):
    out_ref[...] = low(mxu(dy_ref[...], down_w[...], NN) * slope_ref[...])


def unit_kernel(
    first, x_ref, mean_ref, inverse_ref, dqkv_ref, dpre_ref, vec_ref, bias_ref, w_qkv, w_up,
    out_1, out_2, out_3, out_0, sum_ref, result, split_ref,
):
    step = pl.program_id(0)

    @pl.when(step == 0)
    def _():
        split_ref[:, :768] = jnp.sum(wide(dqkv_ref[...]), axis=0, keepdims=True)
        split_ref[:, 768:1792] = jnp.sum(wide(dpre_ref[...]), axis=0, keepdims=True)
        split_ref[:, 1792:] = jnp.zeros((1, 256), f32)

    unit = (wide(x_ref[...]) - mean_ref[...]) * inverse_ref[...]
    one = mxu(dqkv_ref[...], w_qkv[...], NT)
    two = mxu(dpre_ref[...], w_up[...], NT)
    result[...] = low(one * vec_ref[0:1, :] + two * vec_ref[2:3, :])
    sum_ref[0:1, :] = jnp.sum(one * unit, axis=0, keepdims=True)
    sum_ref[1:2, :] = jnp.sum(one, axis=0, keepdims=True)
    sum_ref[2:3, :] = jnp.sum(two * unit, axis=0, keepdims=True)
    sum_ref[3:4, :] = jnp.sum(two, axis=0, keepdims=True)
    sum_ref[4:5, :] = bias_ref[...]
    sum_ref[5:6, :] = split_ref[:, pl.ds(pl.multiple_of(step * 512, 512), 512)]
    sum_ref[6:8, :] = jnp.zeros((2, 512), f32)
    for number, ref in enumerate((out_1, out_2, out_3, out_0)):
        start = pl.multiple_of((first[0] + number) % 4 * 256, 256)
        ref[...] = result[pl.ds(start, 256), :]


def column_grads_kernel(places, att_ref, hidden_ref, d0, d1, d2, d3, o0, o1, o2, o3, far_ref, near_ref):
    step = pl.program_id(0)
    down = low(
        mxu(hidden_ref[...], jnp.concatenate([d0[...], d1[...], d2[...], d3[...]], axis=1), NN)
    )
    out = low(mxu(att_ref[...], jnp.concatenate([o0[...], o1[...], o2[...], o3[...]], axis=1), NN))
    for when, ref in ((step < 2, far_ref), (step >= 2, near_ref)):

        @pl.when(when)
        def _():
            for k in range(4):
                ref[k, :1024] = down[:, k * 128 : k * 128 + 128]
                ref[k, 1024:] = out[:, k * 128 : k * 128 + 128]


def row_grads_kernel(places, a0, a1, a2, a3, b0, b1, b2, b3, dqkv_ref, dpre_ref, far_ref, near_ref):
    step = pl.program_id(0)
    qkv = low(mxu(jnp.concatenate([a0[...], a1[...], a2[...], a3[...]], axis=0), dqkv_ref[...], NN))
    up = low(mxu(jnp.concatenate([b0[...], b1[...], b2[...], b3[...]], axis=0), dpre_ref[...], NN))
    for when, ref in ((step < 2, far_ref), (step >= 2, near_ref)):

        @pl.when(when)
        def _():
            for k in range(4):
                ref[k, :, :768] = qkv[k * 128 : k * 128 + 128]
                ref[k, :, 768:] = up[k * 128 : k * 128 + 128]


def fixed(*shape):
    return pl.BlockSpec(shape, lambda i, *_: (0,) * len(shape))


def led(kernel, steps, lead, ins, in_specs, outs, out_specs, scratch, flops, moved):
    return pl.pallas_call(
        kernel,
        name=kernel.__name__,
        grid_spec=pltpu.PrefetchScalarGridSpec(
            num_scalar_prefetch=1,
            grid=(steps,),
            in_specs=in_specs,
            out_specs=out_specs,
            scratch_shapes=scratch,
        ),
        out_shape=outs,
        compiler_params=pltpu.CompilerParams(vmem_limit_bytes=60 * 2**20),
        cost_estimate=pl.CostEstimate(flops=flops, bytes_accessed=moved, transcendentals=0),
    )(lead, *ins)


def run_norm(tokens, shared_vec):
    return run(
        norm_kernel,
        4,
        (tokens, shared_vec),
        [tiled(256, 2048), whole(6, 2048)],
        [struct((ROWS, 2048), bf16)] * 2
        + [struct((2048, ROWS), bf16)] * 2
        + [struct((ROWS, 1), f32)] * 2,
        [tiled(256, 2048)] * 2
        + [pl.BlockSpec((2048, 256), lambda i: (0, i))] * 2
        + [tiled(256, 1)] * 2,
        [],
        2**24,
        20 * 2**20,
    )


def run_qkv(places, h_one, near, far, bias, table):
    return run(
        qkv_kernel,
        ROWS // TILE,
        (places, h_one, near, far, bias, table),
        [SCALARS, tiled(TILE, 2048), ANY, ANY, whole(1, 768), tiled(TILE, 128)],
        [struct((ROWS, 256), bf16)] * 3 + [struct((2048, 768), bf16)],
        [tiled(TILE, 256)] * 3 + [ANY],
        [pltpu.VMEM((2048, 768), bf16), pltpu.SemaphoreType.DMA((16,)), pltpu.SemaphoreType.DMA],
        2 * ROWS * 2048 * 768,
        9 * 2**20,
    )


def run_place(places, order, near, far, blocks):
    dma = pltpu.SemaphoreType.DMA
    shapes = ((256, 2048), (2048, 1024))
    return run(
        place_kernel,
        1,
        (places, order, near, far, blocks),
        [SCALARS, SCALARS, ANY, ANY, ANY],
        [struct(shape, bf16) for shape in shapes],
        [ANY] * 2,
        [pltpu.VMEM(shape, bf16) for shape in shapes] + [dma((32,)), dma((16,)), dma((2,))],
        1,
        10 * 2**20,
    )


def run_place_down(order, blocks):
    dma = pltpu.SemaphoreType.DMA
    return run(
        place_down_kernel,
        1,
        (order, blocks),
        [SCALARS, ANY],
        struct((2048, 1024), bf16),
        ANY,
        [pltpu.VMEM((2048, 1024), bf16), dma((16,)), dma],
        1,
        8 * 2**20,
    )


def run_up(h_two, w_up, bias):
    return run(
        up_kernel,
        ROWS // TILE,
        (h_two, w_up, bias),
        [tiled(TILE, 2048), whole(2048, 1024), whole(1, 1024)],
        [struct((ROWS, 1024), bf16), struct((ROWS, 1024), f32), struct((1024, ROWS), bf16)],
        [tiled(TILE, 1024)] * 2 + [pl.BlockSpec((1024, TILE), lambda i: (0, i))],
        [],
        2 * ROWS * 2048 * 1024,
        16 * 2**20,
    )


def run_attention(lens, query, key, value, far_key, far_value, cotangent, w_out, table):
    return run(
        attention_kernel,
        ROWS // TILE,
        (lens, query, key, value, far_key, far_value, cotangent, w_out, table),
        [SCALARS, tiled(TILE, 256)]
        + [whole(ROWS, 256)] * 4
        + [tiled(TILE, 2048), whole(256, 2048), tiled(TILE, 128)],
        [struct((ROWS, 256), bf16), struct((256, ROWS), bf16), struct((ROWS, 256), bf16)]
        + [struct((2, ROWS, 256), f32)]
        + [struct((ROWS, 256), bf16)] * 2,
        [tiled(TILE, 256), pl.BlockSpec((256, TILE), lambda i: (0, i)), tiled(TILE, 256)]
        + [whole(2, ROWS, 256)]
        + [whole(ROWS, 256)] * 2,
        [pltpu.VMEM((2, 256, 2 * ROWS), bf16), pltpu.VMEM((2, 2 * ROWS, 256), f32)],
        8 * 2**30,
        12 * 2**20,
    )


def run_branch(attended, hidden, w_out, w_down):
    return run(
        branch_kernel,
        ROWS // TILE,
        (attended, hidden, w_out, w_down),
        [tiled(TILE, 256), tiled(TILE, 1024), whole(256, 2048), whole(2048, 1024)],
        struct((ROWS, 2048), bf16),
        tiled(TILE, 2048),
        [],
        2 * ROWS * 2048 * 1280,
        12 * 2**20,
    )


def run_slope(cotangent, w_down, slope):
    return run(
        slope_kernel,
        ROWS // TILE,
        (cotangent, w_down, slope),
        [tiled(TILE, 2048), whole(2048, 1024), tiled(TILE, 1024)],
        struct((ROWS, 1024), bf16),
        tiled(TILE, 1024),
        [],
        2 * ROWS * 2048 * 1024,
        14 * 2**20,
    )


def run_finish(grad_query, grad_kv, far_gkey, far_gvalue, table):
    kv_spec = pl.BlockSpec((2, 512, 256), lambda i: (0, i, 0))
    return run(
        finish_kernel,
        2,
        (grad_query, grad_kv, far_gkey, far_gvalue, table),
        [tiled(512, 256), kv_spec] + [tiled(512, 256)] * 2 + [tiled(512, 128)],
        struct((ROWS, 768), bf16),
        tiled(512, 768),
        [],
        2**20,
        6 * 2**20,
    )


def run_unit(first, tokens, mean, inverse, grad_qkv, grad_pre, shared_vec, bias_sum, w_qkv, w_up):
    def chunk(rows):
        return pl.BlockSpec((rows, 512), lambda i, lead: (0, i))

    return led(
        unit_kernel,
        4,
        first,
        (tokens, mean, inverse, grad_qkv, grad_pre, shared_vec, bias_sum, w_qkv, w_up),
        [chunk(ROWS), fixed(ROWS, 1), fixed(ROWS, 1), fixed(ROWS, 768), fixed(ROWS, 1024), chunk(6), chunk(1)]
        + [pl.BlockSpec((512, width), lambda i, lead: (i, 0)) for width in (768, 1024)],
        [struct((256, 2048), bf16)] * 4 + [struct((8, 2048), f32)],
        [chunk(256)] * 4 + [chunk(8)],
        [pltpu.VMEM((ROWS, 512), bf16), pltpu.VMEM((1, 2048), f32)],
        2 * ROWS * 2048 * 1792,
        20 * 2**20,
    )


def run_column_grads(places, att_flip, hidden_flip, cotangent):
    def block(which, k):
        return pl.BlockSpec((ROWS, 128), lambda i, p: (0, p[which, (i * 4 + 8 + k) % 16]))

    return led(
        column_grads_kernel,
        4,
        places,
        (att_flip, hidden_flip) + (cotangent,) * 8,
        [fixed(256, ROWS), fixed(1024, ROWS)]
        + [block(3, k) for k in range(4)]
        + [block(1, k) for k in range(4)],
        [struct((8, 1280, 128), bf16)] * 2,
        [
            pl.BlockSpec((4, 1280, 128), lambda i, p: (jnp.minimum(i, 1), 0, 0)),
            pl.BlockSpec((4, 1280, 128), lambda i, p: (jnp.maximum(i - 2, 0), 0, 0)),
        ],
        [],
        2 * ROWS * 2048 * 1280,
        12 * 2**20,
    )


def run_row_grads(places, one_flip, two_flip, grad_qkv, grad_pre):
    def block(which, k):
        return pl.BlockSpec((128, ROWS), lambda i, p: (p[which, (i * 4 + 8 + k) % 16], 0))

    return led(
        row_grads_kernel,
        4,
        places,
        (one_flip,) * 4 + (two_flip,) * 4 + (grad_qkv, grad_pre),
        [block(0, k) for k in range(4)]
        + [block(2, k) for k in range(4)]
        + [fixed(ROWS, 768), fixed(ROWS, 1024)],
        [struct((8, 128, 1792), bf16)] * 2,
        [
            pl.BlockSpec((4, 128, 1792), lambda i, p: (jnp.minimum(i, 1), 0, 0)),
            pl.BlockSpec((4, 128, 1792), lambda i, p: (jnp.maximum(i - 2, 0), 0, 0)),
        ],
        [],
        2 * ROWS * 2048 * 1792,
        16 * 2**20,
    )


def lay_kernel(starts, *refs):
    ins, out, hold, in_sems, out_sems = refs[:-4], refs[-4], refs[-3], refs[-2], refs[-1]
    inward, outward = [], []
    low = 0
    for k, ref in enumerate(ins):
        size = ref.shape[0]
        spot = hold.at[pl.ds(low, size)]
        low += size
        target = out.at[pl.ds(pl.multiple_of(starts[k] * 128, 128), size)]
        inward.append(pltpu.make_async_copy(ref, spot, in_sems.at[k]))
        outward.append(pltpu.make_async_copy(spot, target, out_sems.at[k]))
    for copy in inward:
        copy.start()
    for first, second in zip(inward, outward):
        first.wait()
        second.start()
    for copy in outward:
        copy.wait()


def copy_kernel(source, out, hold_ref, in_sems, out_sems):
    inward, outward = [], []
    for k in range(8):
        spot = pl.ds(k * 128, 128)
        inward.append(pltpu.make_async_copy(source.at[spot], hold_ref.at[spot], in_sems.at[k]))
        outward.append(pltpu.make_async_copy(hold_ref.at[spot], out.at[spot], out_sems.at[k]))
    for copy in inward:
        copy.start()
    for first, second in zip(inward, outward):
        first.wait()
        second.start()
    for copy in outward:
        copy.wait()


def copy_rows(field):
    return pl.pallas_call(
        copy_kernel,
        name="copy_kernel",
        out_shape=struct(field.shape, field.dtype),
        in_specs=[ANY],
        out_specs=ANY,
        scratch_shapes=[
            pltpu.VMEM(field.shape, field.dtype),
            pltpu.SemaphoreType.DMA((8,)),
            pltpu.SemaphoreType.DMA((8,)),
        ],
        compiler_params=pltpu.CompilerParams(vmem_limit_bytes=32 * 2**20),
    )(field)


def lay_rows(starts, pieces, base=None):
    width, dtype = pieces[0].shape[1], pieces[0].dtype
    amount = len(pieces)
    rows = sum(piece.shape[0] for piece in pieces)
    extra = [] if base is None else [base]

    def kernel(starts_ref, *refs):
        lay_kernel(starts_ref, *refs[:amount], *refs[amount + len(extra) :])

    return pl.pallas_call(
        kernel,
        name="lay_kernel",
        out_shape=struct((ROWS, width), dtype),
        in_specs=[SCALARS] + [ANY] * (amount + len(extra)),
        out_specs=ANY,
        scratch_shapes=[
            pltpu.VMEM((rows, width), dtype),
            pltpu.SemaphoreType.DMA((amount,)),
            pltpu.SemaphoreType.DMA((amount,)),
        ],
        input_output_aliases={} if base is None else {1 + amount: 0},
        compiler_params=pltpu.CompilerParams(vmem_limit_bytes=32 * 2**20),
    )(starts, *pieces, *extra)


def up_y(values):
    return lax.ppermute(values, "y", UP)


def down_y(values):
    return lax.ppermute(values, "y", DOWN)


def up_x(values):
    return lax.ppermute(values, "x", UP)


def down_x(values):
    return lax.ppermute(values, "x", DOWN)


def swap(values, axis):
    return lax.ppermute(values, axis, PAIR)


def hold(values):
    return lax.optimization_barrier(values)


def join(*parts):
    return jnp.concatenate(parts, axis=0)


def soap_moments(gradient, first_moment, second_moment, left_basis, right_basis):
    turned = exact_dot(exact_dot(left_basis.T, gradient), right_basis)
    first_new = beta_one * first_moment + (1.0 - beta_one) * turned
    second_new = beta_two * second_moment + (1.0 - beta_two) * turned * turned
    direction = (
        first_new
        / (1.0 - beta_one**STEP)
        / (jnp.sqrt(second_new / (1.0 - beta_two**STEP)) + adam_eps)
    )
    return (exact_dot(left_basis, direction), first_new, second_new)


def soap_weight(state, weight, left_basis, right_basis, step_rate):
    returned = exact_dot(state[0], right_basis.T)
    return (weight * (1.0 - step_rate * weight_decay) - step_rate * returned, state[1], state[2])


def per_device(
    tokens,
    cotangent,
    seq_lens,
    owners,
    shared_vec,
    shared_first,
    shared_second,
    split_vec,
    split_first,
    split_second,
    qkv_master,
    qkv_first,
    qkv_second,
    qkv_left,
    qkv_right,
    out_master,
    out_first,
    out_second,
    out_left,
    out_right,
    up_master,
    up_first,
    up_second,
    up_left,
    up_right,
    down_master,
    down_first,
    down_second,
    down_left,
    down_right,
):
    part = lax.axis_index("s")
    x, z = lax.axis_index("x"), lax.axis_index("z")

    out_block = out_master.reshape(256, 128)
    packed = low(jnp.concatenate([qkv_master[0], out_block[:128], out_block[128:]], axis=1))[None]
    partner = swap(packed, "s")
    up_blocks = lax.all_gather(low(up_master), GROUP_AXES, axis=0, tiled=True)
    down_own = low(down_master.reshape(1024, 128).T)[None]
    lens = jnp.stack([seq_lens[0, 0] // 2, seq_lens[0, 1] // 2, part.astype(jnp.int32)])
    local_index = jnp.arange(ROWS, dtype=jnp.int32)
    _, position = row_places(seq_lens[0, 0], seq_lens[0, 1], part, local_index, 2)
    partner, tokens, lens, position = hold((partner, tokens, lens, position))
    h_one, h_two, one_flip, two_flip, mean, inverse = run_norm(tokens, shared_vec)
    bias_sum = jnp.sum(wide(cotangent), axis=0, keepdims=True) * 0.125
    pair = join(packed, partner)
    before, after = up_y(pair), down_y(pair)
    slots = group_slots()
    ids = jnp.arange(16, dtype=jnp.int32)
    places = jnp.sum(
        jnp.where(owners[:, None, :] == slots[None, :, None], ids[None, None, :], 0), axis=2
    )
    order = jnp.sum(jnp.where(owners[2:, None, :] == ids[None, :, None], ids, 0), axis=2)
    frequency = 10000.0 ** (-2.0 * jnp.arange(32, dtype=f32) / 64)
    angles = position.astype(f32)[:, None] * frequency[None, :]
    cosine, sine_part = jnp.cos(angles), jnp.sin(angles)
    table = jnp.concatenate([cosine, cosine, -sine_part, sine_part], axis=1)
    bias_qkv, bias_up = split_vec[:, :768], split_vec[:, 768:]

    (
        before, after, h_one, h_two, one_flip, two_flip, mean, inverse, places, order, lens, table, bias_qkv, bias_up, bias_sum,
    ) = hold((
        before, after, h_one, h_two, one_flip, two_flip, mean, inverse, places, order, lens, table, bias_qkv, bias_up, bias_sum,
    ))
    far_a, far_b = up_y(before[0:1]), down_y(after[1:2])
    far_a, far_b = hold((far_a, far_b))
    near = join(pair, after, far_a, far_b, before)
    far = swap(near, "c")
    query, key, value, w_qkv = run_qkv(places, h_one, near, far, bias_qkv, table)
    far_key = lax.ppermute(key, "s", [(0, 1)])
    far_value = lax.ppermute(value, "s", [(0, 1)])
    up_blocks, down_own, h_two, query = hold((up_blocks, down_own, h_two, query))
    down_blocks = lax.all_gather(down_own, GROUP_AXES, axis=0, tiled=True)
    w_out, w_up = run_place(places, order, near, far, up_blocks)
    hidden, slope, hidden_flip = run_up(h_two, w_up, bias_up)
    far_key, far_value, hidden, slope, hidden_flip = hold(
        (far_key, far_value, hidden, slope, hidden_flip)
    )
    attended, att_flip, grad_query, grad_kv, far_gkey, far_gvalue = run_attention(
        lens, query, key, value, far_key, far_value, cotangent, w_out, table
    )
    attended, far_gkey, far_gvalue = hold((attended, far_gkey, far_gvalue))
    far_gkey = lax.ppermute(far_gkey, "s", [(1, 0)])
    far_gvalue = lax.ppermute(far_gvalue, "s", [(1, 0)])
    w_down = run_place_down(order, down_blocks)
    partial_out = run_branch(attended, hidden, w_out, w_down)
    partial_out, far_gkey, far_gvalue, slope = hold((partial_out, far_gkey, far_gvalue, slope))
    part_sum = lax.psum_scatter(partial_out, "x", scatter_dimension=0, tiled=True)
    grad_pre = run_slope(cotangent, w_down, slope)
    grad_pre, grad_query = hold((grad_pre, grad_query))
    grad_qkv = run_finish(grad_query, grad_kv, far_gkey, far_gvalue, table)
    row_far, row_near = run_row_grads(places, one_flip, two_flip, grad_qkv, grad_pre)
    row_far, row_near, grad_qkv, grad_pre = hold((row_far, row_near, grad_qkv, grad_pre))
    rows = (row_near, swap(row_far, "c"))

    def both(pair, start, stop):
        return wide(pair[0][start:stop]) + wide(pair[1][start:stop])

    def first_hop(pair):
        return up_y(low(both(pair, 4, 5))), down_y(low(both(pair, 5, 6)))

    def second_hop(pair, first, last):
        ahead = up_y(low(join(both(pair, 2, 3) + wide(first), both(pair, 3, 4))))
        behind = down_y(low(join(both(pair, 6, 7), both(pair, 7, 8) + wide(last))))
        return ahead, behind

    def last_hop(pair, ahead, behind):
        total = both(pair, 0, 2) + wide(ahead) + wide(behind)
        return total[0] + wide(swap(low(total[1]), "s"))

    unit_1, unit_2, unit_3, unit_0, sums = run_unit(
        jnp.stack([x + 1]).astype(jnp.int32),
        tokens,
        mean,
        inverse,
        grad_qkv,
        grad_pre,
        shared_vec,
        bias_sum,
        w_qkv,
        w_up,
    )

    def own(values_in):
        return wide(lax.dynamic_slice_in_dim(values_in, (x * 2 + z) * 128, 128, axis=0))

    def half(values, which):
        return lax.dynamic_slice_in_dim(values, which * 128, 128, axis=0)

    def both_rows(mine, theirs):
        return join(jnp.where(z == 0, mine, theirs), jnp.where(z == 0, theirs, mine))

    near_y = [(i, i ^ 1) for i in range(4)]
    far_y = [(i, i ^ 2) for i in range(4)]

    unit_1, unit_2, unit_3, unit_0, sums, rows, part_sum, hidden_flip = hold(
        (unit_1, unit_2, unit_3, unit_0, sums, rows, part_sum, hidden_flip)
    )
    unit_1, unit_3 = up_x(unit_1), down_x(unit_3)
    row_a, row_b = first_hop(rows)
    out_partner = swap(half(part_sum, 1 - z), "z")
    column_far, column_near = run_column_grads(places, att_flip, hidden_flip, cotangent)
    unit_1, unit_3, row_a, row_b, out_partner, sums, column_far, column_near = hold(
        (unit_1, unit_3, row_a, row_b, out_partner, sums, column_far, column_near)
    )
    unit_2 = lax.ppermute(unit_2, "x", far_y)
    row_prev, row_next = second_hop(rows, row_a, row_b)
    columns = (column_near, swap(column_far, "c"))
    out_rows = low(
        own(tokens) + wide(half(part_sum, z)) + wide(out_partner) + shared_vec[4] + shared_vec[5]
    )
    out_twin = swap(out_rows, "z")
    total = wide(unit_0) + wide(unit_1) + wide(unit_3)
    unit_2, total, row_prev, row_next, columns, out_rows, out_twin, sums = hold(
        (unit_2, total, row_prev, row_next, columns, out_rows, out_twin, sums)
    )
    output = lax.all_gather(both_rows(out_rows, out_twin), "x", axis=0, tiled=True)
    total = total + wide(unit_2)
    own_grad = half(total, z) + wide(swap(low(half(total, 1 - z)), "z"))
    row_sum = last_hop(rows, row_prev, row_next)
    column_a, column_b = first_hop(columns)
    sums = sums + swap(sums, "c")
    own_grad, row_sum, column_a, column_b, sums = hold(
        (own_grad, row_sum, column_a, column_b, sums)
    )
    own_inverse = lax.dynamic_slice_in_dim(inverse, (x * 2 + z) * 128, 128, axis=0)
    own_mean = lax.dynamic_slice_in_dim(mean, (x * 2 + z) * 128, 128, axis=0)
    own_unit = (own(tokens) - own_mean) * own_inverse
    grad_x = (
        own_grad
        - jnp.mean(own_grad, axis=-1, keepdims=True)
        - own_unit * jnp.mean(own_grad * own_unit, axis=-1, keepdims=True)
    ) * own_inverse
    grad_rows = low(own(cotangent) + grad_x)
    grad_twin = swap(grad_rows, "z")
    column_prev, column_next = second_hop(columns, column_a, column_b)
    sums = sums + swap(sums, "s")
    sums = sums + lax.ppermute(sums, "y", near_y)
    new_up = soap_block(
        row_sum[:, 768:], up_master[0], up_first[0], up_second[0], up_left[0, 0], up_right[0, 0], rate_up
    )
    grad_rows, grad_twin, row_sum, column_prev, column_next, sums, new_up = hold(
        (grad_rows, grad_twin, row_sum, column_prev, column_next, sums, new_up)
    )
    grad_pair = both_rows(grad_rows, grad_twin)
    grad_before, grad_after = up_x(grad_pair), down_x(grad_pair)
    column_sum = last_hop(columns, column_prev, column_next)
    sums = sums + lax.ppermute(sums, "y", far_y)
    shared_sum = sums + swap(sums, "z")
    new_qkv = soap_block(
        row_sum[:, :768],
        qkv_master[0],
        qkv_first[0],
        qkv_second[0],
        qkv_left[0, 0],
        qkv_right[0, 0],
        rate_qkv,
    )
    down_state = soap_moments(
        column_sum[:1024], down_first[:, 0], down_second[:, 0], down_left[0, 0], down_right[0, 0]
    )
    new_out = soap_block(
        column_sum[1024:],
        out_master[:, 0],
        out_first[:, 0],
        out_second[:, 0],
        out_left[0, 0],
        out_right[0, 0],
        rate_out,
    )
    grad_before, grad_after, grad_pair, shared_sum, new_qkv, new_out, down_state, output = hold(
        (grad_before, grad_after, grad_pair, shared_sum, new_qkv, new_out, down_state, output)
    )
    far_a, far_b = up_x(grad_before[:128]), down_x(grad_after[128:])
    shared_sum = shared_sum + lax.ppermute(shared_sum, "x", near_y)
    shared_sum = shared_sum + lax.ppermute(shared_sum, "x", far_y)
    output = copy_rows(output)
    spots = jnp.stack([x * 2, ((x + 1) % 4) * 2, ((x + 3) % 4) * 2])
    grad_input = lay_rows(spots, [grad_pair, grad_after, grad_before])
    new_down = soap_weight(
        down_state, down_master[:, 0], down_left[0, 0], down_right[0, 0], rate_down
    )
    far_a, far_b, shared_sum, output, new_down, grad_input = hold(
        (far_a, far_b, shared_sum, output, new_down, grad_input)
    )
    spots = jnp.stack([((x + 2) % 4) * 2, ((x + 2) % 4) * 2 + 1])
    grad_input = lay_rows(spots, [far_a, far_b], grad_input)
    split_grad = sums[5:6, :1792]
    shared_grad = join(shared_sum[:5], shared_sum[4:5])
    new_shared = adam_vector(shared_grad, shared_vec, shared_first, shared_second)
    new_split = adam_vector(split_grad, split_vec, split_first, split_second)
    return (
        output,
        grad_input,
        new_shared[0],
        new_shared[1],
        new_shared[2],
        new_split[0],
        new_split[1],
        new_split[2],
        new_qkv[0][None],
        new_qkv[1][None],
        new_qkv[2][None],
        new_qkv[0][None].astype(bf16),
        new_out[0][:, None],
        new_out[1][:, None],
        new_out[2][:, None],
        new_out[0][:, None].astype(bf16),
        new_up[0][None],
        new_up[1][None],
        new_up[2][None],
        new_up[0][None].astype(bf16),
        new_down[0][:, None],
        new_down[1][:, None],
        new_down[2][:, None],
        new_down[0][:, None].astype(bf16),
    )


def solution(mesh):
    in_specs = (
        P(("y", "c", "s"), None),
        P(("y", "c", "s"), None),
        P(("y", "c"), None),
        P(),
        P(),
        P(),
        P(),
        P(("x", "z"), None),
        P(("x", "z"), None),
        P(("x", "z"), None),
        P(("y", "c", "s"), None, ("x", "z")),
        P(("y", "c", "s"), None, ("x", "z")),
        P(("y", "c", "s"), None, ("x", "z")),
        P(("y", "c", "s"), ("x", "z"), None, None),
        P(("y", "c", "s"), ("x", "z"), None, None),
        P(("x", "z"), ("y", "c", "s"), None),
        P(("x", "z"), ("y", "c", "s"), None),
        P(("x", "z"), ("y", "c", "s"), None),
        P(("y", "c", "s"), ("x", "z"), None, None),
        P(("y", "c", "s"), ("x", "z"), None, None),
        P(("y", "c", "s"), None, ("x", "z")),
        P(("y", "c", "s"), None, ("x", "z")),
        P(("y", "c", "s"), None, ("x", "z")),
        P(("y", "c", "s"), ("x", "z"), None, None),
        P(("y", "c", "s"), ("x", "z"), None, None),
        P(("x", "z"), ("y", "c", "s"), None),
        P(("x", "z"), ("y", "c", "s"), None),
        P(("x", "z"), ("y", "c", "s"), None),
        P(("y", "c", "s"), ("x", "z"), None, None),
        P(("y", "c", "s"), ("x", "z"), None, None),
    )
    out_specs = (
        P(("y", "c", "s"), None),
        P(("y", "c", "s"), None),
        P(),
        P(),
        P(),
        P(("x", "z"), None),
        P(("x", "z"), None),
        P(("x", "z"), None),
        P(("y", "c", "s"), None, ("x", "z")),
        P(("y", "c", "s"), None, ("x", "z")),
        P(("y", "c", "s"), None, ("x", "z")),
        P(("y", "c", "s"), None, ("x", "z")),
        P(("x", "z"), ("y", "c", "s"), None),
        P(("x", "z"), ("y", "c", "s"), None),
        P(("x", "z"), ("y", "c", "s"), None),
        P(("x", "z"), ("y", "c", "s"), None),
        P(("y", "c", "s"), None, ("x", "z")),
        P(("y", "c", "s"), None, ("x", "z")),
        P(("y", "c", "s"), None, ("x", "z")),
        P(("y", "c", "s"), None, ("x", "z")),
        P(("x", "z"), ("y", "c", "s"), None),
        P(("x", "z"), ("y", "c", "s"), None),
        P(("x", "z"), ("y", "c", "s"), None),
        P(("x", "z"), ("y", "c", "s"), None),
    )
    fine = Mesh(mesh.devices.reshape(4, 2, 2, 4, 2), ("y", "c", "s", "x", "z"))
    return jax.shard_map(
        per_device, mesh=fine, in_specs=in_specs, out_specs=out_specs, check_vma=False
    )
```
